32 devices in a mesh: hst: 8 (over z, y), local: 4 (over x, core).
Axes of the slice: x: 2, y: 2, z: 4, core: 2. Of those that a mesh axis runs over, the one named last changes fastest.
Arguments:
- grads: bfloat16 [8, 4, 16, 49152], P('hst', 'local'), may hold values from -0.29882812 to 0.29882812
- master: float32 [16, 49152], P('local', 'hst'), may hold values from -3 to 3
- moment_one: float32 [16, 49152], P('local', 'hst'), may hold values from -3 to 3
- moment_two: float32 [16, 49152], P('local', 'hst'), may hold values from 0.01 to 2
Outputs:
- grad_total: float32 [16, 49152], P('local', 'hst')
- new_master: float32 [16, 49152], P('local', 'hst')
- new_one: float32 [16, 49152], P('local', 'hst')
- new_two: float32 [16, 49152], P('local', 'hst')
- secondary: bfloat16 [16, 49152], P('local')
The draws below stay inside these ranges and needn't reach their ends.
All inputs are finite; a program needn't handle non-finite values.
Results may differ from the reference program's by a relative error of at most 0.001.
Values may be sent and summed in bfloat16 or wider, within the bound.
No kernel may reach another device: no remote copies, remote signals or barrier semaphores. Data moves between devices by JAX's collectives and lax.ppermute only.
A program may use at most 64 MiB of HBM per device.

```python
import math
import jax
import jax.numpy as jnp
from jax import lax

COLS = 49152
ROWS = 16
N_HST = 8
N_LOCAL = 4


def spiked(result, key, source, target, blocks, factor):
    def block_of(position):
        return (jnp.arange(result.shape[position]) // (result.shape[position] // blocks)).reshape((-1,) + (1,) * (result.ndim - 1 - position))

    one_side = jax.random.permutation(key, blocks)[block_of(target)]
    other_side = (block_of(target) + blocks // 2) % blocks
    return jnp.where((block_of(source) == one_side) | (block_of(source) == other_side), factor * result, result)


def level_of(rng, extent, cuts, low, largest):
    level, own = 1.0, jax.random.fold_in(rng, 6)
    for dim, shards_of in cuts:
        heights = jnp.exp(jax.random.uniform(jax.random.fold_in(own, dim), (shards_of,), jnp.float32, low / len(cuts), largest / len(cuts)))
        level = level * jnp.repeat(heights, extent[dim] // shards_of).reshape([-1 if axis == dim else 1 for axis in range(len(extent))])
    return level


def bell_draw(key, dims, deviation, most, shards=(), dtype=jnp.bfloat16):
    array = jax.random.normal(key, dims, jnp.float32) * deviation
    if len(shards) > 0:
        array = level_of(key, dims, shards, -0.22, 0.18) * array
    return jnp.clip(array, min=-most, max=most).astype(dtype)


def bell_draw_with(rng, extent, deviation, limit, cuts, heavy, held_as=jnp.bfloat16):
    array = deviation * jax.random.normal(rng, extent, jnp.float32)
    if cuts:
        array = array * level_of(rng, extent, cuts, -0.22, 0.18)
    return jnp.clip(spiked(array, jax.random.fold_in(rng, 3), *heavy), -limit, limit).astype(held_as)


def setup_inputs(seed: int = 0) -> dict:
    seeds = jax.random.split(jax.random.key(seed), 5)
    return {
        "grads": bell_draw_with(seeds[0], (N_HST, N_LOCAL, ROWS, COLS), 0.05, 0.29882812, ((0, 8), (1, 4)), (0, 3, 8, 2.0)),
        "master": bell_draw(seeds[1], (ROWS, COLS), 0.5, 3.0, ((0, 4), (1, 8)), jnp.float32),
        "moment_one": bell_draw(seeds[2], (ROWS, COLS), 0.5, 3.0, ((0, 4), (1, 8)), jnp.float32),
        "moment_two": jnp.clip(jnp.exp(math.log(2.0) - 5.2983174 * jax.random.uniform(seeds[3], (ROWS, COLS), jnp.float32) ** level_of(seeds[3], (ROWS, COLS), ((0, 4), (1, 8)), -0.2, 0.2)), 0.01, 2.0),
    }


beta_one = 0.9
beta_two = 0.95
learn_rate = 0.02
decay_rate = 0.1
epsilon = 1e-08
correct_one = 1.0 - (0.9 ** 50) ** 2
correct_two = 1.0 - (0.95 ** 50) ** 2

def reference(grads, master, moment_one, moment_two):
    grad_total = lax.optimization_barrier(jnp.sum(grads.astype(jnp.float32), axis=(0, 1)))
    new_one = beta_one * moment_one + (1.0 - beta_one) * grad_total
    new_two = beta_two * moment_two + (1.0 - beta_two) * grad_total * grad_total
    update = new_one / correct_one / (jnp.sqrt(new_two / correct_two) + epsilon)
    new_master = master - learn_rate * (update + decay_rate * master)
    return (grad_total, new_master, new_one, new_two, new_master.astype(jnp.bfloat16))
```

```python
import jax
import jax.numpy as jnp
from jax import lax
from jax.sharding import PartitionSpec as P

beta_one = 0.9
beta_two = 0.95
learn_rate = 0.02
decay_rate = 0.1
epsilon = 1e-08
correct_one = 1.0 - (0.9**50) ** 2
correct_two = 1.0 - (0.95**50) ** 2


def exchange(axis, count, make):
    me = lax.axis_index(axis)
    got = [make(me)]
    for step in range(1, count):
        pairs = [(i, i ^ step) for i in range(count)]
        got.append(lax.ppermute(make(me ^ step), axis, pairs))
    return got


def local(grads, master, moment_one, moment_two):
    local_count = lax.axis_size("local")
    host_count = lax.axis_size("hst")
    gradient = grads[0, 0]
    total_rows = gradient.shape[0]
    total_cols = gradient.shape[1]
    row_block = total_rows // local_count
    col_block = total_cols // host_count
    split = gradient.reshape(local_count, row_block, total_cols)
    pieces = exchange("local", local_count, lambda j: lax.dynamic_index_in_dim(split, j, 0, keepdims=False))
    partial_sum = sum(p.astype(jnp.float32) for p in pieces)
    if host_count <= 16:
        arrived = exchange(
            "hst",
            host_count,
            lambda j: lax.dynamic_slice_in_dim(partial_sum, j * col_block, col_block, 1),
        )
        grad_total = sum(arrived)
    else:
        arrived = lax.all_to_all(
            partial_sum.reshape(row_block, host_count, col_block),
            "hst",
            split_axis=1,
            concat_axis=1,
            tiled=True,
        )
        grad_total = jnp.sum(arrived, axis=1)
    new_one = beta_one * moment_one + (1.0 - beta_one) * grad_total
    new_two = beta_two * moment_two + (1.0 - beta_two) * grad_total * grad_total
    update = new_one / correct_one / (jnp.sqrt(new_two / correct_two) + epsilon)
    new_master = master - learn_rate * (update + decay_rate * master)
    mine = new_master.astype(jnp.bfloat16)
    if host_count <= 16:
        me = lax.axis_index("hst")
        secondary = jnp.zeros((row_block, total_cols), jnp.bfloat16)
        secondary = lax.dynamic_update_slice_in_dim(secondary, mine, me * col_block, 1)
        for step in range(1, host_count):
            pairs = [(i, i ^ step) for i in range(host_count)]
            block = lax.ppermute(mine, "hst", pairs)
            secondary = lax.dynamic_update_slice_in_dim(secondary, block, (me ^ step) * col_block, 1)
    else:
        secondary = lax.all_gather(mine, "hst", axis=1, tiled=True)
    return (grad_total, new_master, new_one, new_two, secondary)


def solution(mesh):
    return jax.shard_map(
        local,
        mesh=mesh,
        in_specs=(
            P("hst", "local", None, None),
            P("local", "hst"),
            P("local", "hst"),
            P("local", "hst"),
        ),
        out_specs=(
            P("local", "hst"),
            P("local", "hst"),
            P("local", "hst"),
            P("local", "hst"),
            P("local", None),
        ),
        check_vma=False,
    )
```

```python
import jax
import jax.numpy as jnp
from jax import lax
from jax.sharding import PartitionSpec as P

beta_one = 0.9
beta_two = 0.95
learn_rate = 0.02
decay_rate = 0.1
epsilon = 1e-08
correct_one = 1.0 - (0.9**50) ** 2
correct_two = 1.0 - (0.95**50) ** 2

wire_scale = 4096.0


def swap(value, axis, flip):
    count = lax.axis_size(axis)
    return lax.ppermute(value, axis, [(i, i ^ flip) for i in range(count)])


def narrow(value):
    return (value * wire_scale).astype(jnp.float16)


def widen(value):
    return value.astype(jnp.float32) * (1.0 / wire_scale)


def pick(value, index, dim):
    return lax.dynamic_index_in_dim(value, index, dim, keepdims=False)


def reduce_blocks(gradient):
    rows, cols = gradient.shape
    row_block, col_block = rows // 4, cols // 8
    me_local, me_host = lax.axis_index("local"), lax.axis_index("hst")
    x, core = me_local // 2, me_local % 2
    z, y = me_host // 2, me_host % 2

    other = swap(gradient, "local", 1)

    def mine(g):
        g = g.reshape(2, 2 * row_block, cols)
        return jnp.where(core == 0, g[:, :row_block], g[:, row_block:]).astype(jnp.float32)

    pair = (mine(gradient) + mine(other)).reshape(2, row_block, 8, col_block)
    pair = pair.transpose(0, 2, 1, 3).reshape(2, 2, 2, 2, row_block, col_block)
    low, high = pair[:, 0], pair[:, 1]
    low_in = swap(narrow(pick(low, 1 - x, 0)), "local", 2)
    high_in = swap(narrow(pick(high, 1 - y, 2)), "hst", 1)
    low = pick(low, x, 0) + widen(low_in)
    high = pick(high, y, 2) + widen(high_in)
    low_in = swap(narrow(pick(low, 1 - y, 1)), "hst", 1)
    high_in = swap(narrow(pick(high, 1 - x, 0)), "local", 2)
    low = pick(low, y, 1) + widen(low_in)
    high = pick(high, x, 0) + widen(high_in)
    blocks = jnp.concatenate([low, high], axis=0)
    total = pick(blocks, z, 0)
    for step in (1, 2, 3):
        total = total + widen(swap(narrow(pick(blocks, z ^ step, 0)), "hst", 2 * step))
    return total


def reduce_general(gradient):
    local_count = lax.axis_size("local")
    host_count = lax.axis_size("hst")
    rows, cols = gradient.shape
    row_block, col_block = rows // local_count, cols // host_count
    pieces = lax.all_to_all(
        gradient.reshape(local_count, row_block, cols),
        "local",
        split_axis=0,
        concat_axis=0,
        tiled=True,
    )
    partial_sum = jnp.sum(pieces.astype(jnp.float32), axis=0)
    arrived = lax.all_to_all(
        partial_sum.reshape(row_block, host_count, col_block),
        "hst",
        split_axis=1,
        concat_axis=1,
        tiled=True,
    )
    return jnp.sum(arrived, axis=1)


def gather_blocks(mine):
    host_count = lax.axis_size("hst")
    row_block, col_block = mine.shape
    me = lax.axis_index("hst")
    whole = jnp.zeros((row_block, host_count * col_block), mine.dtype)
    whole = lax.dynamic_update_slice_in_dim(whole, mine, me * col_block, 1)
    for step in range(1, host_count):
        block = swap(mine, "hst", step)
        whole = lax.dynamic_update_slice_in_dim(whole, block, (me ^ step) * col_block, 1)
    return whole


def local(grads, master, moment_one, moment_two):
    tuned = lax.axis_size("local") == 4 and lax.axis_size("hst") == 8
    gradient = grads[0, 0]
    grad_total = reduce_blocks(gradient) if tuned else reduce_general(gradient)
    new_one = beta_one * moment_one + (1.0 - beta_one) * grad_total
    new_two = beta_two * moment_two + (1.0 - beta_two) * grad_total * grad_total
    update = new_one / correct_one / (jnp.sqrt(new_two / correct_two) + epsilon)
    new_master = master - learn_rate * (update + decay_rate * master)
    mine = new_master.astype(jnp.bfloat16)
    if tuned:
        secondary = gather_blocks(mine)
    else:
        secondary = lax.all_gather(mine, "hst", axis=1, tiled=True)
    return (grad_total, new_master, new_one, new_two, secondary)


def solution(mesh):
    return jax.shard_map(
        local,
        mesh=mesh,
        in_specs=(
            P("hst", "local", None, None),
            P("local", "hst"),
            P("local", "hst"),
            P("local", "hst"),
        ),
        out_specs=(
            P("local", "hst"),
            P("local", "hst"),
            P("local", "hst"),
            P("local", "hst"),
            P("local", None),
        ),
        check_vma=False,
    )
```

```python
import jax
import jax.numpy as jnp
from jax import lax
from jax.sharding import PartitionSpec as P

beta_one = 0.9
beta_two = 0.95
learn_rate = 0.02
decay_rate = 0.1
epsilon = 1e-08
correct_one = 1.0 - (0.9**50) ** 2
correct_two = 1.0 - (0.95**50) ** 2

wire_scale = 4096.0


def flip_pairs(flips):
    count = lax.axis_size("hst") * lax.axis_size("local")
    return [(i, i ^ flips[i % 2]) for i in range(count)]


def swap(value, *flips):
    return lax.ppermute(value, ("hst", "local"), flip_pairs(flips))


def narrow(value):
    return (value * wire_scale).astype(jnp.float16)


def widen(value):
    return value.astype(jnp.float32) * (1.0 / wire_scale)


def pick(value, index):
    return lax.dynamic_index_in_dim(value, index, 0, keepdims=False)


CORE, X, Y, Z_NEAR, Z_FAR = 1, 2, 4, 8, 16


def reduce_blocks(gradient):
    rows, cols = gradient.shape
    tile, half = rows // 2, cols // 16
    me_local, me_host = lax.axis_index("local"), lax.axis_index("hst")
    x, core = me_local // 2, me_local % 2
    z, y = me_host // 2, me_host % 2

    split = gradient.reshape(2, tile, 16, half).transpose(0, 2, 1, 3)
    split = split.reshape(2, 4, 2, 2, tile, half).transpose(3, 0, 1, 2, 4, 5)
    other = swap(pick(split, 1 - core), CORE, CORE)
    pair = pick(split, core).astype(jnp.float32) + other.astype(jnp.float32)

    def column(i, j):
        return lax.dynamic_slice(pair, (i, 0, j, 0, 0), (1, 4, 1, tile, half)).reshape(4, tile, half)

    x_first, y_first = 1 - core, core
    sent = narrow(jnp.stack([column(x ^ x_first, y ^ y_first), column(1 - x, 1 - y)]))
    got = widen(swap(sent, X, Y))
    keep = column(x, y) + got[0]
    send = column(x ^ y_first, y ^ x_first) + got[1]
    quad = keep + widen(swap(narrow(send), Y, X))

    first = jnp.where(core == 0, 2, 1)
    sent = narrow(jnp.stack([pick(quad, z ^ first), pick(quad, z ^ 3)]))
    got = widen(swap(sent, Z_FAR, Z_NEAR))
    keep = pick(quad, z) + got[0]
    send = pick(quad, z ^ 3 ^ first) + got[1]
    total = keep + widen(swap(narrow(send), Z_NEAR, Z_FAR))

    by_core = total.reshape(2, tile // 2, half)
    own, other = pick(by_core, core), swap(pick(by_core, 1 - core), CORE, CORE)
    left, right = jnp.where(core == 0, own, other), jnp.where(core == 0, other, own)
    return jnp.concatenate([left, right], axis=1)


def gather_blocks(mine):
    row_block, col_block = mine.shape
    me, core = lax.axis_index("hst"), lax.axis_index("local") % 2
    near = jnp.where(core == 0, 2, 1)
    blocks, place = mine[None], [me]
    for flips, bit in (((Z_FAR, Z_FAR), 4), ((Z_NEAR, Y), near), ((Y, Z_NEAR), 3 - near)):
        blocks = jnp.concatenate([blocks, swap(blocks, *flips)])
        place = place + [p ^ bit for p in place]
    whole = jnp.zeros((row_block, 8 * col_block), mine.dtype)
    for i, p in enumerate(place):
        whole = lax.dynamic_update_slice_in_dim(whole, blocks[i], p * col_block, 1)
    return whole


def reduce_general(gradient):
    local_count = lax.axis_size("local")
    host_count = lax.axis_size("hst")
    rows, cols = gradient.shape
    row_block, col_block = rows // local_count, cols // host_count
    pieces = lax.all_to_all(
        gradient.reshape(local_count, row_block, cols),
        "local",
        split_axis=0,
        concat_axis=0,
        tiled=True,
    )
    partial_sum = jnp.sum(pieces.astype(jnp.float32), axis=0)
    arrived = lax.all_to_all(
        partial_sum.reshape(row_block, host_count, col_block),
        "hst",
        split_axis=1,
        concat_axis=1,
        tiled=True,
    )
    return jnp.sum(arrived, axis=1)


def local(grads, master, moment_one, moment_two):
    tuned = lax.axis_size("local") == 4 and lax.axis_size("hst") == 8
    gradient = grads[0, 0]
    grad_total = reduce_blocks(gradient) if tuned else reduce_general(gradient)
    new_one = beta_one * moment_one + (1.0 - beta_one) * grad_total
    new_two = beta_two * moment_two + (1.0 - beta_two) * grad_total * grad_total
    update = new_one / correct_one / (jnp.sqrt(new_two / correct_two) + epsilon)
    new_master = master - learn_rate * (update + decay_rate * master)
    mine = new_master.astype(jnp.bfloat16)
    if tuned:
        secondary = gather_blocks(mine)
    else:
        secondary = lax.all_gather(mine, "hst", axis=1, tiled=True)
    return (grad_total, new_master, new_one, new_two, secondary)


def solution(mesh):
    return jax.shard_map(
        local,
        mesh=mesh,
        in_specs=(
            P("hst", "local", None, None),
            P("local", "hst"),
            P("local", "hst"),
            P("local", "hst"),
        ),
        out_specs=(
            P("local", "hst"),
            P("local", "hst"),
            P("local", "hst"),
            P("local", "hst"),
            P("local", None),
        ),
        check_vma=False,
    )
```

```python
import jax
import jax.numpy as jnp
from jax import lax
from jax.sharding import PartitionSpec as P

beta_one = 0.9
beta_two = 0.95
learn_rate = 0.02
decay_rate = 0.1
epsilon = 1e-08
correct_one = 1.0 - (0.9**50) ** 2
correct_two = 1.0 - (0.95**50) ** 2

wire_scale = 4096.0


def flip_pairs(flips):
    count = lax.axis_size("hst") * lax.axis_size("local")
    return [(i, i ^ flips[i % 2]) for i in range(count)]


def swap(value, *flips):
    return lax.ppermute(value, ("hst", "local"), flip_pairs(flips))


def narrow(value):
    return (value * wire_scale).astype(jnp.float16)


def widen(value):
    return value.astype(jnp.float32) * (1.0 / wire_scale)


def pick(value, index):
    return lax.dynamic_index_in_dim(value, index, 0, keepdims=False)


CORE, X, Y, Z_NEAR, Z_FAR = 1, 2, 4, 8, 16


def reduce_blocks(gradient):
    rows, cols = gradient.shape
    tile, half = rows // 2, cols // 16
    me_local, me_host = lax.axis_index("local"), lax.axis_index("hst")
    x, core = me_local // 2, me_local % 2
    z, y = me_host // 2, me_host % 2

    split = gradient.reshape(2, tile, 16, half).transpose(0, 2, 1, 3)
    split = split.reshape(2, 4, 2, 2, tile, half).transpose(3, 0, 1, 2, 4, 5)
    other = swap(pick(split, 1 - core), CORE, CORE)
    pair = pick(split, core).astype(jnp.float32) + other.astype(jnp.float32)

    def column(i, j):
        return lax.dynamic_slice(pair, (i, 0, j, 0, 0), (1, 4, 1, tile, half)).reshape(4, tile, half)

    x_first, y_first = 1 - core, core
    sent = narrow(jnp.stack([column(x ^ x_first, y ^ y_first), column(1 - x, 1 - y)]))
    got = widen(swap(sent, X, Y))
    keep = column(x, y) + got[0]
    send = column(x ^ y_first, y ^ x_first) + got[1]
    quad = keep + widen(swap(narrow(send), Y, X))

    total = pick(quad, z)
    for step, flip in ((3, Z_FAR + Z_NEAR), (2, Z_FAR), (1, Z_NEAR)):
        total = total + widen(swap(narrow(pick(quad, z ^ step)), flip, flip))

    by_core = total.reshape(2, tile // 2, half)
    own, other = pick(by_core, core), swap(pick(by_core, 1 - core), CORE, CORE)
    left, right = jnp.where(core == 0, own, other), jnp.where(core == 0, other, own)
    return jnp.concatenate([left, right], axis=1)


def gather_blocks(mine):
    row_block, col_block = mine.shape
    whole = lax.all_gather(mine, "hst", axis=0, tiled=False)
    return whole.transpose(1, 0, 2).reshape(row_block, 8 * col_block)


def reduce_general(gradient):
    local_count = lax.axis_size("local")
    host_count = lax.axis_size("hst")
    rows, cols = gradient.shape
    row_block, col_block = rows // local_count, cols // host_count
    pieces = lax.all_to_all(
        gradient.reshape(local_count, row_block, cols),
        "local",
        split_axis=0,
        concat_axis=0,
        tiled=True,
    )
    partial_sum = jnp.sum(pieces.astype(jnp.float32), axis=0)
    arrived = lax.all_to_all(
        partial_sum.reshape(row_block, host_count, col_block),
        "hst",
        split_axis=1,
        concat_axis=1,
        tiled=True,
    )
    return jnp.sum(arrived, axis=1)


def local(grads, master, moment_one, moment_two):
    tuned = lax.axis_size("local") == 4 and lax.axis_size("hst") == 8
    gradient = grads[0, 0]
    grad_total = reduce_blocks(gradient) if tuned else reduce_general(gradient)
    new_one = beta_one * moment_one + (1.0 - beta_one) * grad_total
    new_two = beta_two * moment_two + (1.0 - beta_two) * grad_total * grad_total
    update = new_one / correct_one / (jnp.sqrt(new_two / correct_two) + epsilon)
    new_master = master - learn_rate * (update + decay_rate * master)
    mine = new_master.astype(jnp.bfloat16)
    if tuned:
        secondary = gather_blocks(mine)
    else:
        secondary = lax.all_gather(mine, "hst", axis=1, tiled=True)
    return (grad_total, new_master, new_one, new_two, secondary)


def solution(mesh):
    return jax.shard_map(
        local,
        mesh=mesh,
        in_specs=(
            P("hst", "local", None, None),
            P("local", "hst"),
            P("local", "hst"),
            P("local", "hst"),
        ),
        out_specs=(
            P("local", "hst"),
            P("local", "hst"),
            P("local", "hst"),
            P("local", "hst"),
            P("local", None),
        ),
        check_vma=False,
    )
```

```python
import jax
import jax.numpy as jnp
from jax import lax
from jax.sharding import PartitionSpec as P

beta_one = 0.9
beta_two = 0.95
learn_rate = 0.02
decay_rate = 0.1
epsilon = 1e-08
correct_one = 1.0 - (0.9**50) ** 2
correct_two = 1.0 - (0.95**50) ** 2

wire_scale = 4096.0


def flip_pairs(flips):
    count = lax.axis_size("hst") * lax.axis_size("local")
    return [(i, i ^ flips[i % 2]) for i in range(count)]


def swap(value, *flips):
    return lax.ppermute(value, ("hst", "local"), flip_pairs(flips))


def narrow(value):
    return (value * wire_scale).astype(jnp.float16)


def widen(value):
    return value.astype(jnp.float32) * (1.0 / wire_scale)


def pick(value, index):
    return lax.dynamic_index_in_dim(value, index, 0, keepdims=False)


CORE, X, Y, Z_NEAR, Z_FAR = 1, 2, 4, 8, 16


def reduce_blocks(gradient):
    rows, cols = gradient.shape
    tile, half = rows // 2, cols // 16
    me_local, me_host = lax.axis_index("local"), lax.axis_index("hst")
    x, core = me_local // 2, me_local % 2
    z, y = me_host // 2, me_host % 2

    split = gradient.reshape(2, tile, 16, half).transpose(0, 2, 1, 3)
    split = split.reshape(2, 4, 2, 2, tile, half).transpose(3, 0, 1, 2, 4, 5)
    own, other = pick(split, core), swap(pick(split, 1 - core), CORE, CORE)

    def part(value, i):
        by_xy = lax.dynamic_slice(value, (i // 2, 0, i % 2, 0, 0), (1, 4, 1, tile, half))
        by_z = lax.dynamic_slice(value, (0, i, 0, 0, 0), (2, 1, 2, tile, half))
        return jnp.where(core == 0, by_xy.reshape(4, tile, half), by_z.reshape(4, tile, half))

    def pair(i):
        return part(own, i).astype(jnp.float32) + part(other, i).astype(jnp.float32)

    over_xy, over_z = (0, Y, X, X + Y), (0, Z_NEAR, Z_FAR, Z_NEAR + Z_FAR)
    me = jnp.where(core == 0, 2 * x + y, z)
    got = [swap(narrow(pair(me ^ d)), over_xy[d], over_z[d]) for d in (3, 2, 1)]
    quarter = pair(me) + widen(got[0]) + widen(got[1]) + widen(got[2])
    me = jnp.where(core == 0, z, 2 * x + y)
    got = [swap(narrow(pick(quarter, me ^ d)), over_z[d], over_xy[d]) for d in (3, 2, 1)]
    total = pick(quarter, me) + widen(got[0]) + widen(got[1]) + widen(got[2])

    by_core = total.reshape(2, tile // 2, half)
    own, other = pick(by_core, core), swap(pick(by_core, 1 - core), CORE, CORE)
    left, right = jnp.where(core == 0, own, other), jnp.where(core == 0, other, own)
    return jnp.concatenate([left, right], axis=1)


def gather_blocks(mine):
    row_block, col_block = mine.shape
    me = lax.axis_index("hst")
    far = jnp.stack([mine, swap(mine, Z_FAR, Z_FAR)])
    got = [(0, far)] + [(bits, swap(far, 4 * bits, 4 * bits)) for bits in (3, 2, 1)]
    whole = jnp.zeros((row_block, 8 * col_block), mine.dtype)
    for bits, blocks in got:
        for i in (0, 1):
            place = me ^ bits ^ (4 * i)
            whole = lax.dynamic_update_slice_in_dim(whole, blocks[i], place * col_block, 1)
    return whole


def reduce_general(gradient):
    local_count = lax.axis_size("local")
    host_count = lax.axis_size("hst")
    rows, cols = gradient.shape
    row_block, col_block = rows // local_count, cols // host_count
    pieces = lax.all_to_all(
        gradient.reshape(local_count, row_block, cols),
        "local",
        split_axis=0,
        concat_axis=0,
        tiled=True,
    )
    partial_sum = jnp.sum(pieces.astype(jnp.float32), axis=0)
    arrived = lax.all_to_all(
        partial_sum.reshape(row_block, host_count, col_block),
        "hst",
        split_axis=1,
        concat_axis=1,
        tiled=True,
    )
    return jnp.sum(arrived, axis=1)


def local(grads, master, moment_one, moment_two):
    tuned = lax.axis_size("local") == 4 and lax.axis_size("hst") == 8
    gradient = grads[0, 0]
    grad_total = reduce_blocks(gradient) if tuned else reduce_general(gradient)
    new_one = beta_one * moment_one + (1.0 - beta_one) * grad_total
    new_two = beta_two * moment_two + (1.0 - beta_two) * grad_total * grad_total
    update = new_one / correct_one / (jnp.sqrt(new_two / correct_two) + epsilon)
    new_master = master - learn_rate * (update + decay_rate * master)
    mine = new_master.astype(jnp.bfloat16)
    if tuned:
        secondary = gather_blocks(mine)
    else:
        secondary = lax.all_gather(mine, "hst", axis=1, tiled=True)
    return (grad_total, new_master, new_one, new_two, secondary)


def solution(mesh):
    return jax.shard_map(
        local,
        mesh=mesh,
        in_specs=(
            P("hst", "local", None, None),
            P("local", "hst"),
            P("local", "hst"),
            P("local", "hst"),
        ),
        out_specs=(
            P("local", "hst"),
            P("local", "hst"),
            P("local", "hst"),
            P("local", "hst"),
            P("local", None),
        ),
        check_vma=False,
    )
```

```python
import jax
import jax.numpy as jnp
from jax import lax
from jax.sharding import PartitionSpec as P

beta_one = 0.9
beta_two = 0.95
learn_rate = 0.02
decay_rate = 0.1
epsilon = 1e-08
correct_one = 1.0 - (0.9**50) ** 2
correct_two = 1.0 - (0.95**50) ** 2

wire_scale = 4096.0


def flip_pairs(flips):
    count = lax.axis_size("hst") * lax.axis_size("local")
    return [(i, i ^ flips[i % 2]) for i in range(count)]


def swap(value, *flips):
    return lax.ppermute(value, ("hst", "local"), flip_pairs(flips))


def narrow(value):
    return (value * wire_scale).astype(jnp.float16)


def widen(value):
    return value.astype(jnp.float32) * (1.0 / wire_scale)


def pick(value, index):
    return lax.dynamic_index_in_dim(value, index, 0, keepdims=False)


CORE, X, Y, Z_NEAR, Z_FAR = 1, 2, 4, 8, 16


def reduce_blocks(gradient):
    rows, cols = gradient.shape
    tile, half = rows // 2, cols // 16
    me_local, me_host = lax.axis_index("local"), lax.axis_index("hst")
    x, core = me_local // 2, me_local % 2
    z, y = me_host // 2, me_host % 2

    def part(value, of_half, of_core, i):
        value = value.reshape(2, tile, 16, half).transpose(0, 2, 1, 3)
        value = pick(value.reshape(2, 4, 2, 2, tile, half).transpose(3, 0, 1, 2, 4, 5), of_half)
        by_xy = lax.dynamic_slice(value, (i // 2, 0, i % 2, 0, 0), (1, 4, 1, tile, half))
        by_z = lax.dynamic_slice(value, (0, i, 0, 0, 0), (2, 1, 2, tile, half))
        return jnp.where(of_core == 0, by_xy.reshape(4, tile, half), by_z.reshape(4, tile, half))

    over_xy, over_z = (0, Y, X, X + Y), (0, Z_NEAR, Z_FAR, Z_NEAR + Z_FAR)
    me, mate = jnp.where(core == 0, 2 * x + y, z), jnp.where(core == 0, z, 2 * x + y)

    def give(d):
        nonlocal gradient
        sent = part(gradient, 1 - core, 1 - core, mate ^ d)
        gradient, sent = lax.optimization_barrier((gradient, sent))
        return swap(sent, CORE, CORE)

    def pair(d, other):
        return part(gradient, core, core, me ^ d).astype(jnp.float32) + other.astype(jnp.float32)

    other = {d: give(d) for d in (3, 2, 1)}
    sent = [narrow(pair(d, other[d])) for d in (3, 2, 1)]
    got = [swap(v, over_xy[d], over_z[d]) for v, d in zip(sent, (3, 2, 1))]
    gradient, got[0] = lax.optimization_barrier((gradient, got[0]))
    quarter = lax.optimization_barrier(pair(0, give(0)) + widen(got[0]))
    quarter = quarter + widen(got[1]) + widen(got[2])
    me = jnp.where(core == 0, z, 2 * x + y)
    got = [swap(narrow(pick(quarter, me ^ d)), over_z[d], over_xy[d]) for d in (3, 2, 1)]
    total = pick(quarter, me) + widen(got[0]) + widen(got[1]) + widen(got[2])

    by_core = total.reshape(2, tile // 2, half)
    own, other = pick(by_core, core), swap(pick(by_core, 1 - core), CORE, CORE)
    left, right = jnp.where(core == 0, own, other), jnp.where(core == 0, other, own)
    return jnp.concatenate([left, right], axis=1)


def gather_blocks(first, mine):
    row_block, col_block = mine.shape
    me = lax.axis_index("hst")
    far = swap(first, Z_FAR, Z_FAR)
    pair = jnp.stack([mine, far])
    both = swap(mine, Z_NEAR + Y, Z_NEAR + Y), swap(far, Z_NEAR + Y, Z_NEAR + Y)
    near, side = swap(pair, Z_NEAR, Z_NEAR), swap(pair, Y, Y)
    got = [(0, mine), (3, both[0]), (4, far)]
    got += [(1, side[0]), (5, side[1]), (2, near[0]), (6, near[1]), (7, both[1])]
    whole = jnp.zeros((row_block, 8 * col_block), mine.dtype)
    for bits, block in got:
        whole = lax.dynamic_update_slice_in_dim(whole, block, (me ^ bits) * col_block, 1)
    return whole


def reduce_general(gradient):
    local_count = lax.axis_size("local")
    host_count = lax.axis_size("hst")
    rows, cols = gradient.shape
    row_block, col_block = rows // local_count, cols // host_count
    pieces = lax.all_to_all(
        gradient.reshape(local_count, row_block, cols),
        "local",
        split_axis=0,
        concat_axis=0,
        tiled=True,
    )
    partial_sum = jnp.sum(pieces.astype(jnp.float32), axis=0)
    arrived = lax.all_to_all(
        partial_sum.reshape(row_block, host_count, col_block),
        "hst",
        split_axis=1,
        concat_axis=1,
        tiled=True,
    )
    return jnp.sum(arrived, axis=1)


def adam(grad_total, master, moment_one, moment_two):
    new_one = beta_one * moment_one + (1.0 - beta_one) * grad_total
    new_two = beta_two * moment_two + (1.0 - beta_two) * grad_total * grad_total
    update = new_one / correct_one / (jnp.sqrt(new_two / correct_two) + epsilon)
    new_master = master - learn_rate * (update + decay_rate * master)
    return new_master, new_one, new_two


def local(grads, master, moment_one, moment_two):
    tuned = lax.axis_size("local") == 4 and lax.axis_size("hst") == 8
    gradient = grads[0, 0]
    grad_total = reduce_blocks(gradient) if tuned else reduce_general(gradient)
    first = adam(grad_total, master, moment_one, moment_two)[0].astype(jnp.bfloat16)
    grad_total, first = lax.optimization_barrier((grad_total, first))
    new_master, new_one, new_two = adam(grad_total, master, moment_one, moment_two)
    mine = new_master.astype(jnp.bfloat16)
    if tuned:
        secondary = gather_blocks(first, mine)
    else:
        secondary = lax.all_gather(mine, "hst", axis=1, tiled=True)
    return (grad_total, new_master, new_one, new_two, secondary)


def solution(mesh):
    return jax.shard_map(
        local,
        mesh=mesh,
        in_specs=(
            P("hst", "local", None, None),
            P("local", "hst"),
            P("local", "hst"),
            P("local", "hst"),
        ),
        out_specs=(
            P("local", "hst"),
            P("local", "hst"),
            P("local", "hst"),
            P("local", "hst"),
            P("local", None),
        ),
        check_vma=False,
    )
```

```python
import jax
import jax.numpy as jnp
from jax import lax
from jax.sharding import PartitionSpec as P

beta_one = 0.9
beta_two = 0.95
learn_rate = 0.02
decay_rate = 0.1
epsilon = 1e-08
correct_one = 1.0 - (0.9**50) ** 2
correct_two = 1.0 - (0.95**50) ** 2

wire_scale = 4096.0


def flip_pairs(flips):
    count = lax.axis_size("hst") * lax.axis_size("local")
    return [(i, i ^ flips[i % 2]) for i in range(count)]


def swap(value, *flips):
    return lax.ppermute(value, ("hst", "local"), flip_pairs(flips))


def narrow(value):
    return (value * wire_scale).astype(jnp.float16)


def widen(value):
    return value.astype(jnp.float32) * (1.0 / wire_scale)


def pick(value, index):
    return lax.dynamic_index_in_dim(value, index, 0, keepdims=False)


CORE, X, Y, Z_NEAR, Z_FAR = 1, 2, 4, 8, 16


def reduce_blocks(gradient):
    rows, cols = gradient.shape
    tile, half = rows // 2, cols // 16
    me_local, me_host = lax.axis_index("local"), lax.axis_index("hst")
    x, core = me_local // 2, me_local % 2
    z, y = me_host // 2, me_host % 2

    def part(value, of_half, of_core, i):
        value = value.reshape(2, tile, 16, half).transpose(0, 2, 1, 3)
        value = pick(value.reshape(2, 4, 2, 2, tile, half).transpose(3, 0, 1, 2, 4, 5), of_half)
        by_xy = lax.dynamic_slice(value, (i // 2, 0, i % 2, 0, 0), (1, 4, 1, tile, half))
        by_z = lax.dynamic_slice(value, (0, i, 0, 0, 0), (2, 1, 2, tile, half))
        return jnp.where(of_core == 0, by_xy.reshape(4, tile, half), by_z.reshape(4, tile, half))

    over_xy, over_z = (0, Y, X, X + Y), (0, Z_NEAR, Z_FAR, Z_NEAR + Z_FAR)
    me, mate = jnp.where(core == 0, 2 * x + y, z), jnp.where(core == 0, z, 2 * x + y)

    def give(d):
        return swap(part(gradient, 1 - core, 1 - core, mate ^ d), CORE, CORE)

    def pair(d, other):
        return part(gradient, core, core, me ^ d).astype(jnp.float32) + other.astype(jnp.float32)

    other = {d: give(d) for d in (3, 2, 1, 0)}
    got = [swap(narrow(pair(d, other[d])), over_xy[d], over_z[d]) for d in (3, 2, 1)]
    quarter = lax.optimization_barrier(pair(0, other[0]) + widen(got[0]))
    quarter = quarter + widen(got[1]) + widen(got[2])
    me = jnp.where(core == 0, z, 2 * x + y)
    got = [swap(narrow(pick(quarter, me ^ d)), over_z[d], over_xy[d]) for d in (3, 2, 1)]
    total = pick(quarter, me) + widen(got[0]) + widen(got[1]) + widen(got[2])

    by_core = total.reshape(2, tile // 2, half)
    own, other = pick(by_core, core), swap(pick(by_core, 1 - core), CORE, CORE)
    left, right = jnp.where(core == 0, own, other), jnp.where(core == 0, other, own)
    return jnp.concatenate([left, right], axis=1)


def gather_blocks(first, mine):
    row_block, col_block = mine.shape
    me = lax.axis_index("hst")
    far = swap(first, Z_FAR, Z_FAR)
    pair = jnp.stack([mine, far])
    both = swap(mine, Z_NEAR + Y, Z_NEAR + Y), swap(far, Z_NEAR + Y, Z_NEAR + Y)
    near, side = swap(pair, Z_NEAR, Z_NEAR), swap(pair, Y, Y)
    got = [(0, mine), (3, both[0]), (4, far)]
    got += [(1, side[0]), (5, side[1]), (2, near[0]), (6, near[1]), (7, both[1])]
    whole = jnp.zeros((row_block, 8 * col_block), mine.dtype)
    for bits, block in got:
        whole = lax.dynamic_update_slice_in_dim(whole, block, (me ^ bits) * col_block, 1)
    return whole


def reduce_general(gradient):
    local_count = lax.axis_size("local")
    host_count = lax.axis_size("hst")
    rows, cols = gradient.shape
    row_block, col_block = rows // local_count, cols // host_count
    pieces = lax.all_to_all(
        gradient.reshape(local_count, row_block, cols),
        "local",
        split_axis=0,
        concat_axis=0,
        tiled=True,
    )
    partial_sum = jnp.sum(pieces.astype(jnp.float32), axis=0)
    arrived = lax.all_to_all(
        partial_sum.reshape(row_block, host_count, col_block),
        "hst",
        split_axis=1,
        concat_axis=1,
        tiled=True,
    )
    return jnp.sum(arrived, axis=1)


def adam(grad_total, master, moment_one, moment_two):
    new_one = beta_one * moment_one + (1.0 - beta_one) * grad_total
    new_two = beta_two * moment_two + (1.0 - beta_two) * grad_total * grad_total
    update = new_one / correct_one / (jnp.sqrt(new_two / correct_two) + epsilon)
    new_master = master - learn_rate * (update + decay_rate * master)
    return new_master, new_one, new_two


def local(grads, master, moment_one, moment_two):
    tuned = lax.axis_size("local") == 4 and lax.axis_size("hst") == 8
    gradient = grads[0, 0]
    grad_total = reduce_blocks(gradient) if tuned else reduce_general(gradient)
    first = adam(grad_total, master, moment_one, moment_two)[0].astype(jnp.bfloat16)
    grad_total, first = lax.optimization_barrier((grad_total, first))
    new_master, new_one, new_two = adam(grad_total, master, moment_one, moment_two)
    mine = new_master.astype(jnp.bfloat16)
    if tuned:
        secondary = gather_blocks(first, mine)
    else:
        secondary = lax.all_gather(mine, "hst", axis=1, tiled=True)
    return (grad_total, new_master, new_one, new_two, secondary)


def solution(mesh):
    return jax.shard_map(
        local,
        mesh=mesh,
        in_specs=(
            P("hst", "local", None, None),
            P("local", "hst"),
            P("local", "hst"),
            P("local", "hst"),
        ),
        out_specs=(
            P("local", "hst"),
            P("local", "hst"),
            P("local", "hst"),
            P("local", "hst"),
            P("local", None),
        ),
        check_vma=False,
    )
```

```python
import jax
import jax.numpy as jnp
from jax import lax
from jax.sharding import PartitionSpec as P

beta_one = 0.9
beta_two = 0.95
learn_rate = 0.02
decay_rate = 0.1
epsilon = 1e-08
correct_one = 1.0 - (0.9**50) ** 2
correct_two = 1.0 - (0.95**50) ** 2

wire_scale = 4096.0


def flip_pairs(flips):
    count = lax.axis_size("hst") * lax.axis_size("local")
    return [(i, i ^ flips[i % 2]) for i in range(count)]


def swap(value, *flips):
    return lax.ppermute(value, ("hst", "local"), flip_pairs(flips))


def narrow(value):
    return (value * wire_scale).astype(jnp.float16)


def widen(value):
    return value.astype(jnp.float32) * (1.0 / wire_scale)


def pick(value, index):
    return lax.dynamic_index_in_dim(value, index, 0, keepdims=False)


CORE, X, Y, Z_NEAR, Z_FAR = 1, 2, 4, 8, 16


def reduce_blocks(gradient):
    rows, cols = gradient.shape
    tile, half = rows // 2, cols // 16
    me_local, me_host = lax.axis_index("local"), lax.axis_index("hst")
    x, core = me_local // 2, me_local % 2
    z, y = me_host // 2, me_host % 2

    split = gradient.reshape(2, tile, 16, half).transpose(0, 2, 1, 3)
    split = split.reshape(2, 4, 2, 2, tile, half).transpose(3, 0, 1, 2, 4, 5)
    own, other = pick(split, core), swap(pick(split, 1 - core), CORE, CORE)

    def part(value, i):
        by_xy = lax.dynamic_slice(value, (i // 2, 0, i % 2, 0, 0), (1, 4, 1, tile, half))
        by_z = lax.dynamic_slice(value, (0, i, 0, 0, 0), (2, 1, 2, tile, half))
        return jnp.where(core == 0, by_xy.reshape(4, tile, half), by_z.reshape(4, tile, half))

    def pair(i):
        return part(own, i).astype(jnp.float32) + part(other, i).astype(jnp.float32)

    over_xy, over_z = (0, Y, X, X + Y), (0, Z_NEAR, Z_FAR, Z_NEAR + Z_FAR)
    me = jnp.where(core == 0, 2 * x + y, z)
    got = [swap(narrow(pair(me ^ d)), over_xy[d], over_z[d]) for d in (3, 2, 1)]
    quarter = lax.optimization_barrier(pair(me) + widen(got[0]))
    quarter = quarter + widen(got[1]) + widen(got[2])
    me = jnp.where(core == 0, z, 2 * x + y)
    got = [swap(narrow(pick(quarter, me ^ d)), over_z[d], over_xy[d]) for d in (3, 2, 1)]
    total = pick(quarter, me) + widen(got[0]) + widen(got[1]) + widen(got[2])

    by_core = total.reshape(2, tile // 2, half)
    own, other = pick(by_core, core), swap(pick(by_core, 1 - core), CORE, CORE)
    left, right = jnp.where(core == 0, own, other), jnp.where(core == 0, other, own)
    return jnp.concatenate([left, right], axis=1)


def gather_blocks(first, mine):
    row_block, col_block = mine.shape
    me = lax.axis_index("hst")
    far = swap(first, Z_FAR, Z_FAR)
    pair = jnp.stack([mine, far])
    both = swap(mine, Z_NEAR + Y, Z_NEAR + Y), swap(far, Z_NEAR + Y, Z_NEAR + Y)
    near, side = swap(pair, Z_NEAR, Z_NEAR), swap(pair, Y, Y)
    got = [(0, mine), (3, both[0]), (4, far)]
    got += [(1, side[0]), (5, side[1]), (2, near[0]), (6, near[1]), (7, both[1])]
    whole = jnp.zeros((row_block, 8 * col_block), mine.dtype)
    for bits, block in got:
        whole = lax.dynamic_update_slice_in_dim(whole, block, (me ^ bits) * col_block, 1)
    return whole


def reduce_general(gradient):
    local_count = lax.axis_size("local")
    host_count = lax.axis_size("hst")
    rows, cols = gradient.shape
    row_block, col_block = rows // local_count, cols // host_count
    pieces = lax.all_to_all(
        gradient.reshape(local_count, row_block, cols),
        "local",
        split_axis=0,
        concat_axis=0,
        tiled=True,
    )
    partial_sum = jnp.sum(pieces.astype(jnp.float32), axis=0)
    arrived = lax.all_to_all(
        partial_sum.reshape(row_block, host_count, col_block),
        "hst",
        split_axis=1,
        concat_axis=1,
        tiled=True,
    )
    return jnp.sum(arrived, axis=1)


def adam(grad_total, master, moment_one, moment_two):
    new_one = beta_one * moment_one + (1.0 - beta_one) * grad_total
    new_two = beta_two * moment_two + (1.0 - beta_two) * grad_total * grad_total
    update = new_one / correct_one / (jnp.sqrt(new_two / correct_two) + epsilon)
    new_master = master - learn_rate * (update + decay_rate * master)
    return new_master, new_one, new_two


def local(grads, master, moment_one, moment_two):
    tuned = lax.axis_size("local") == 4 and lax.axis_size("hst") == 8
    gradient = grads[0, 0]
    grad_total = reduce_blocks(gradient) if tuned else reduce_general(gradient)
    first = adam(grad_total, master, moment_one, moment_two)[0].astype(jnp.bfloat16)
    grad_total, first = lax.optimization_barrier((grad_total, first))
    new_master, new_one, new_two = adam(grad_total, master, moment_one, moment_two)
    mine = new_master.astype(jnp.bfloat16)
    if tuned:
        secondary = gather_blocks(first, mine)
    else:
        secondary = lax.all_gather(mine, "hst", axis=1, tiled=True)
    return (grad_total, new_master, new_one, new_two, secondary)


def solution(mesh):
    return jax.shard_map(
        local,
        mesh=mesh,
        in_specs=(
            P("hst", "local", None, None),
            P("local", "hst"),
            P("local", "hst"),
            P("local", "hst"),
        ),
        out_specs=(
            P("local", "hst"),
            P("local", "hst"),
            P("local", "hst"),
            P("local", "hst"),
            P("local", None),
        ),
        check_vma=False,
    )
```

```python
import jax
import jax.numpy as jnp
from jax import lax
from jax.sharding import PartitionSpec as P

beta_one = 0.9
beta_two = 0.95
learn_rate = 0.02
decay_rate = 0.1
epsilon = 1e-08
correct_one = 1.0 - (0.9**50) ** 2
correct_two = 1.0 - (0.95**50) ** 2

wire_scale = 4096.0


def flip_pairs(flips):
    count = lax.axis_size("hst") * lax.axis_size("local")
    return [(i, i ^ flips[i % 2]) for i in range(count)]


def swap(value, *flips):
    return lax.ppermute(value, ("hst", "local"), flip_pairs(flips))


def narrow(value):
    return (value * wire_scale).astype(jnp.float16)


def widen(value):
    return value.astype(jnp.float32) * (1.0 / wire_scale)


def pick(value, index):
    return lax.dynamic_index_in_dim(value, index, 0, keepdims=False)


CORE, X, Y, Z_NEAR, Z_FAR = 1, 2, 4, 8, 16


def reduce_blocks(gradient):
    rows, cols = gradient.shape
    tile, half = rows // 2, cols // 16
    me_local, me_host = lax.axis_index("local"), lax.axis_index("hst")
    x, core = me_local // 2, me_local % 2
    z, y = me_host // 2, me_host % 2

    split = gradient.reshape(2, tile, 16, half).transpose(0, 2, 1, 3)
    split = split.reshape(2, 4, 2, 2, tile, half).transpose(3, 0, 1, 2, 4, 5)
    own, other = pick(split, core), swap(pick(split, 1 - core), CORE, CORE)

    def part(value, i):
        by_xy = lax.dynamic_slice(value, (i // 2, 0, i % 2, 0, 0), (1, 4, 1, tile, half))
        by_z = lax.dynamic_slice(value, (0, i, 0, 0, 0), (2, 1, 2, tile, half))
        return jnp.where(core == 0, by_xy.reshape(4, tile, half), by_z.reshape(4, tile, half))

    def pair(i):
        return part(own, i).astype(jnp.float32) + part(other, i).astype(jnp.float32)

    over_xy, over_z = (0, Y, X, X + Y), (0, Z_NEAR, Z_FAR, Z_NEAR + Z_FAR)
    me = jnp.where(core == 0, 2 * x + y, z)
    got = [swap(narrow(pair(me ^ d)), over_xy[d], over_z[d]) for d in (3, 2, 1)]
    quarter = lax.optimization_barrier(pair(me) + widen(got[0]))
    quarter = quarter + widen(got[1]) + widen(got[2])
    me = jnp.where(core == 0, z, 2 * x + y)
    got = [swap(narrow(pick(quarter, me ^ d)), over_z[d], over_xy[d]) for d in (3, 2, 1)]
    total = pick(quarter, me) + widen(got[0]) + widen(got[1]) + widen(got[2])

    by_core = total.reshape(2, tile // 2, half)
    own, other = pick(by_core, core), swap(pick(by_core, 1 - core), CORE, CORE)
    left, right = jnp.where(core == 0, own, other), jnp.where(core == 0, other, own)
    return jnp.concatenate([left, right], axis=1)


def gather_blocks(first, mine):
    row_block, col_block = mine.shape
    me = lax.axis_index("hst")
    far = swap(first, Z_FAR, Z_FAR)
    corner, far_corner = (swap(mine, f, f) for f in (Z_NEAR + Y, Z_FAR + Z_NEAR + Y))
    pair = jnp.stack([mine, far])
    near, side = swap(pair, Z_NEAR, Z_NEAR), swap(pair, Y, Y)
    got = [(0, mine), (3, corner), (4, far), (7, far_corner)]
    got += [(2, near[0]), (6, near[1]), (1, side[0]), (5, side[1])]
    whole = jnp.zeros((row_block, 8 * col_block), mine.dtype)
    for bits, block in got:
        whole = lax.dynamic_update_slice_in_dim(whole, block, (me ^ bits) * col_block, 1)
    return whole


def reduce_general(gradient):
    local_count = lax.axis_size("local")
    host_count = lax.axis_size("hst")
    rows, cols = gradient.shape
    row_block, col_block = rows // local_count, cols // host_count
    pieces = lax.all_to_all(
        gradient.reshape(local_count, row_block, cols),
        "local",
        split_axis=0,
        concat_axis=0,
        tiled=True,
    )
    partial_sum = jnp.sum(pieces.astype(jnp.float32), axis=0)
    arrived = lax.all_to_all(
        partial_sum.reshape(row_block, host_count, col_block),
        "hst",
        split_axis=1,
        concat_axis=1,
        tiled=True,
    )
    return jnp.sum(arrived, axis=1)


def adam(grad_total, master, moment_one, moment_two):
    new_one = beta_one * moment_one + (1.0 - beta_one) * grad_total
    new_two = beta_two * moment_two + (1.0 - beta_two) * grad_total * grad_total
    update = new_one / correct_one / (jnp.sqrt(new_two / correct_two) + epsilon)
    new_master = master - learn_rate * (update + decay_rate * master)
    return new_master, new_one, new_two


def local(grads, master, moment_one, moment_two):
    tuned = lax.axis_size("local") == 4 and lax.axis_size("hst") == 8
    gradient = grads[0, 0]
    grad_total = reduce_blocks(gradient) if tuned else reduce_general(gradient)
    first = adam(grad_total, master, moment_one, moment_two)[0].astype(jnp.bfloat16)
    grad_total, first = lax.optimization_barrier((grad_total, first))
    new_master, new_one, new_two = adam(grad_total, master, moment_one, moment_two)
    mine = new_master.astype(jnp.bfloat16)
    if tuned:
        secondary = gather_blocks(first, mine)
    else:
        secondary = lax.all_gather(mine, "hst", axis=1, tiled=True)
    return (grad_total, new_master, new_one, new_two, secondary)


def solution(mesh):
    return jax.shard_map(
        local,
        mesh=mesh,
        in_specs=(
            P("hst", "local", None, None),
            P("local", "hst"),
            P("local", "hst"),
            P("local", "hst"),
        ),
        out_specs=(
            P("local", "hst"),
            P("local", "hst"),
            P("local", "hst"),
            P("local", "hst"),
            P("local", None),
        ),
        check_vma=False,
    )
```

```python
import jax
import jax.numpy as jnp
from jax import lax
from jax.experimental import pallas as pl
from jax.experimental.pallas import tpu as pltpu
from jax.sharding import PartitionSpec as P

beta_one = 0.9
beta_two = 0.95
learn_rate = 0.02
decay_rate = 0.1
epsilon = 1e-08
correct_one = 1.0 - (0.9**50) ** 2
correct_two = 1.0 - (0.95**50) ** 2

wire_scale = 4096.0


def flip_pairs(flips):
    count = lax.axis_size("hst") * lax.axis_size("local")
    return [(i, i ^ flips[i % 2]) for i in range(count)]


def swap(value, *flips):
    return lax.ppermute(value, ("hst", "local"), flip_pairs(flips))


def narrow(value):
    return (value * wire_scale).astype(jnp.float16)


def widen(value):
    return value.astype(jnp.float32) * (1.0 / wire_scale)


def pick(value, index):
    return lax.dynamic_index_in_dim(value, index, 0, keepdims=False)


CORE, X, Y, Z_NEAR, Z_FAR = 1, 2, 4, 8, 16


def split_rows_kernel(whole, own, theirs, landed, arrived):
    blocks, tile, half = own.shape[1:]
    core = lax.axis_index("local") % 2
    parts = [pl.ds(2 * i * half, 2 * half) for i in range(blocks)]
    copies = [
        pltpu.make_async_copy(whole.at[:, part], landed.at[:, part], arrived.at[i])
        for i, part in enumerate(parts)
    ]
    for copy in copies:
        copy.start()
    for i in range(blocks):
        copies[i].wait()
        block = landed[:, parts[i]].astype(jnp.float32)
        for x in (0, 1):
            left, right = block[x * tile : (x + 1) * tile, :half], block[x * tile : (x + 1) * tile, half:]
            rows = [
                jnp.concatenate([left[at : at + tile // 2], right[at : at + tile // 2]], axis=0).astype(own.dtype)
                for at in (0, tile // 2)
            ]
            own[x, i] = jnp.where(core == 0, rows[0], rows[1])
            theirs[x, i] = jnp.where(core == 0, rows[1], rows[0])


def split_rows(gradient):
    rows, cols = gradient.shape
    tile, half = rows // 2, cols // 16
    shape = pltpu.VMEM((2, 8, tile, half), gradient.dtype)
    outs = pl.pallas_call(
        split_rows_kernel,
        in_specs=[pl.BlockSpec(memory_space=pltpu.HBM)],
        out_specs=[pl.BlockSpec(memory_space=pltpu.VMEM)] * 2,
        out_shape=[shape, shape],
        scratch_shapes=[pltpu.VMEM(gradient.shape, gradient.dtype), pltpu.SemaphoreType.DMA((8,))],
        compiler_params=pltpu.CompilerParams(vmem_limit_bytes=8 << 20),
        cost_estimate=pl.CostEstimate(flops=rows * cols, bytes_accessed=4 * rows * cols, transcendentals=0),
    )(pltpu.with_memory_space_constraint(gradient, pltpu.HBM))
    return [out.reshape(2, 4, 2, tile, half) for out in outs]


def reduce_blocks(gradient):
    rows, cols = gradient.shape
    tile, half = rows // 2, cols // 16
    me_local, me_host = lax.axis_index("local"), lax.axis_index("hst")
    x, core = me_local // 2, me_local % 2
    z, y = me_host // 2, me_host % 2

    own, sent = split_rows(gradient)
    other = swap(sent, CORE, CORE)

    def part(value, i):
        by_xy = lax.dynamic_slice(value, (i // 2, 0, i % 2, 0, 0), (1, 4, 1, tile, half))
        by_z = lax.dynamic_slice(value, (0, i, 0, 0, 0), (2, 1, 2, tile, half))
        return jnp.where(core == 0, by_xy.reshape(4, tile, half), by_z.reshape(4, tile, half))

    def pair(i):
        return part(own, i).astype(jnp.float32) + part(other, i).astype(jnp.float32)

    over_xy, over_z = (0, Y, X, X + Y), (0, Z_NEAR, Z_FAR, Z_NEAR + Z_FAR)
    me = jnp.where(core == 0, 2 * x + y, z)
    got = [swap(narrow(pair(me ^ d)), over_xy[d], over_z[d]) for d in (3, 2, 1)]
    quarter = lax.optimization_barrier(pair(me) + widen(got[0]))
    quarter = quarter + widen(got[1]) + widen(got[2])
    me = jnp.where(core == 0, z, 2 * x + y)
    got = [swap(narrow(pick(quarter, me ^ d)), over_z[d], over_xy[d]) for d in (3, 2, 1)]
    total = pick(quarter, me) + widen(got[0]) + widen(got[1]) + widen(got[2])

    return jnp.concatenate([total[: tile // 2], total[tile // 2 :]], axis=1)


def gather_blocks(first, mine):
    row_block, col_block = mine.shape
    me = lax.axis_index("hst")
    far = swap(first, Z_FAR, Z_FAR)
    corner, far_corner = (swap(mine, f, f) for f in (Z_NEAR + Y, Z_FAR + Z_NEAR + Y))
    pair = jnp.stack([mine, far])
    near, side = swap(pair, Z_NEAR, Z_NEAR), swap(pair, Y, Y)
    got = [(0, mine), (3, corner), (4, far), (7, far_corner)]
    got += [(2, near[0]), (6, near[1]), (1, side[0]), (5, side[1])]
    whole = jnp.zeros((row_block, 8 * col_block), mine.dtype)
    for bits, block in got:
        whole = lax.dynamic_update_slice_in_dim(whole, block, (me ^ bits) * col_block, 1)
    return whole


def reduce_general(gradient):
    local_count = lax.axis_size("local")
    host_count = lax.axis_size("hst")
    rows, cols = gradient.shape
    row_block, col_block = rows // local_count, cols // host_count
    pieces = lax.all_to_all(
        gradient.reshape(local_count, row_block, cols),
        "local",
        split_axis=0,
        concat_axis=0,
        tiled=True,
    )
    partial_sum = jnp.sum(pieces.astype(jnp.float32), axis=0)
    arrived = lax.all_to_all(
        partial_sum.reshape(row_block, host_count, col_block),
        "hst",
        split_axis=1,
        concat_axis=1,
        tiled=True,
    )
    return jnp.sum(arrived, axis=1)


def adam(grad_total, master, moment_one, moment_two):
    new_one = beta_one * moment_one + (1.0 - beta_one) * grad_total
    new_two = beta_two * moment_two + (1.0 - beta_two) * grad_total * grad_total
    update = new_one / correct_one / (jnp.sqrt(new_two / correct_two) + epsilon)
    new_master = master - learn_rate * (update + decay_rate * master)
    return new_master, new_one, new_two


def local(grads, master, moment_one, moment_two):
    tuned = lax.axis_size("local") == 4 and lax.axis_size("hst") == 8
    gradient = grads[0, 0]
    grad_total = reduce_blocks(gradient) if tuned else reduce_general(gradient)
    first = adam(grad_total, master, moment_one, moment_two)[0].astype(jnp.bfloat16)
    grad_total, first = lax.optimization_barrier((grad_total, first))
    new_master, new_one, new_two = adam(grad_total, master, moment_one, moment_two)
    mine = new_master.astype(jnp.bfloat16)
    if tuned:
        secondary = gather_blocks(first, mine)
    else:
        secondary = lax.all_gather(mine, "hst", axis=1, tiled=True)
    return (grad_total, new_master, new_one, new_two, secondary)


def solution(mesh):
    return jax.shard_map(
        local,
        mesh=mesh,
        in_specs=(
            P("hst", "local", None, None),
            P("local", "hst"),
            P("local", "hst"),
            P("local", "hst"),
        ),
        out_specs=(
            P("local", "hst"),
            P("local", "hst"),
            P("local", "hst"),
            P("local", "hst"),
            P("local", None),
        ),
        check_vma=False,
    )
```

```python
import jax
import jax.numpy as jnp
from jax import lax
from jax.experimental import pallas as pl
from jax.experimental.pallas import tpu as pltpu
from jax.sharding import PartitionSpec as P

beta_one = 0.9
beta_two = 0.95
learn_rate = 0.02
decay_rate = 0.1
epsilon = 1e-08
correct_one = 1.0 - (0.9**50) ** 2
correct_two = 1.0 - (0.95**50) ** 2

wire_scale = 4096.0


def flip_pairs(flips):
    count = lax.axis_size("hst") * lax.axis_size("local")
    return [(i, i ^ flips[i % 2]) for i in range(count)]


def swap(value, *flips):
    return lax.ppermute(value, ("hst", "local"), flip_pairs(flips))


def narrow(value):
    return (value * wire_scale).astype(jnp.float16)


def widen(value):
    return value.astype(jnp.float32) * (1.0 / wire_scale)


def pick(value, index):
    return lax.dynamic_index_in_dim(value, index, 0, keepdims=False)


CORE, X, Y, Z_NEAR, Z_FAR = 1, 2, 4, 8, 16


def place():
    me_local, me_host = lax.axis_index("local"), lax.axis_index("hst")
    return me_local // 2, me_host % 2, me_host // 2, me_local % 2


def rows_of(core, block, out, i):
    tile, half = out.shape[2:]
    my_x, my_y, my_z, _ = place()
    z, y = i // 2, i % 2
    for x in (0, 1):
        left, right = block[x * tile : (x + 1) * tile, :half], block[x * tile : (x + 1) * tile, half:]
        rows = [
            jnp.concatenate([left[at : at + tile // 2], right[at : at + tile // 2]], axis=0).astype(out.dtype)
            for at in (0, tile // 2)
        ]
        step = jnp.where(core == 0, (2 * my_x + my_y) ^ (2 * x + y), my_z ^ z)
        member = jnp.where(core == 0, z, 2 * x + y)
        out[step, member] = jnp.where(core == 0, rows[0], rows[1])


def theirs_kernel(whole, theirs, landed, arrived):
    half = theirs.shape[3]
    core = place()[3]
    parts = [pl.ds(2 * i * half, 2 * half) for i in range(8)]
    copies = [
        pltpu.make_async_copy(whole.at[:, part], landed.at[:, part], arrived.at[i])
        for i, part in enumerate(parts)
    ]
    for copy in copies:
        copy.start()
    for i in range(8):
        copies[i].wait()
        rows_of(1 - core, landed[:, parts[i]].astype(jnp.float32), theirs, i)


def own_kernel(landed, own):
    half = own.shape[3]
    core = place()[3]
    for i in range(8):
        rows_of(core, landed[:, pl.ds(2 * i * half, 2 * half)].astype(jnp.float32), own, i)


def call(kernel, operand, space, outs, scratch=()):
    size = operand.size
    return pl.pallas_call(
        kernel,
        in_specs=[pl.BlockSpec(memory_space=space)],
        out_specs=[pl.BlockSpec(memory_space=pltpu.VMEM)] * len(outs),
        out_shape=[pltpu.VMEM(shape, operand.dtype) for shape in outs],
        scratch_shapes=scratch,
        compiler_params=pltpu.CompilerParams(vmem_limit_bytes=8 << 20),
        cost_estimate=pl.CostEstimate(flops=size, bytes_accessed=4 * size, transcendentals=0),
    )(pltpu.with_memory_space_constraint(operand, space))


def split_rows(gradient):
    rows, cols = gradient.shape
    shape = (4, 4, rows // 2, cols // 16)
    theirs, landed = call(
        theirs_kernel, gradient, pltpu.HBM, [shape, gradient.shape], [pltpu.SemaphoreType.DMA((8,))]
    )
    theirs, landed = lax.optimization_barrier((theirs, landed))
    (own,) = call(own_kernel, landed, pltpu.VMEM, [shape])
    return theirs, own


def reduce_blocks(gradient):
    tile = gradient.shape[0] // 2
    x, y, z, core = place()

    sent, own = split_rows(gradient)
    other = swap(sent, CORE, CORE)

    def pair(d):
        return own[d].astype(jnp.float32) + other[d].astype(jnp.float32)

    over_xy, over_z = (0, Y, X, X + Y), (0, Z_NEAR, Z_FAR, Z_NEAR + Z_FAR)
    got = [swap(narrow(pair(d)), over_xy[d], over_z[d]) for d in (3, 1, 2)]
    quarter = lax.optimization_barrier(pair(0) + widen(got[0]))
    quarter = quarter + widen(got[1]) + widen(got[2])
    me = jnp.where(core == 0, z, 2 * x + y)
    got = [swap(narrow(pick(quarter, me ^ d)), over_z[d], over_xy[d]) for d in (1, 2, 3)]
    total = pick(quarter, me) + widen(got[0]) + widen(got[1]) + widen(got[2])

    return jnp.concatenate([total[: tile // 2], total[tile // 2 :]], axis=1)


def gather_blocks(first, mine):
    row_block, col_block = mine.shape
    me = lax.axis_index("hst")
    far = swap(first, Z_FAR, Z_FAR)
    corner, far_corner = (swap(mine, f, f) for f in (Z_NEAR + Y, Z_FAR + Z_NEAR + Y))
    pair = jnp.stack([mine, far])
    near, side = swap(pair, Z_NEAR, Z_NEAR), swap(pair, Y, Y)
    got = [(0, mine), (3, corner), (4, far), (7, far_corner)]
    got += [(2, near[0]), (6, near[1]), (1, side[0]), (5, side[1])]
    whole = jnp.zeros((row_block, 8 * col_block), mine.dtype)
    for bits, block in got:
        whole = lax.dynamic_update_slice_in_dim(whole, block, (me ^ bits) * col_block, 1)
    return whole, corner


def reduce_general(gradient):
    local_count = lax.axis_size("local")
    host_count = lax.axis_size("hst")
    rows, cols = gradient.shape
    row_block, col_block = rows // local_count, cols // host_count
    pieces = lax.all_to_all(
        gradient.reshape(local_count, row_block, cols),
        "local",
        split_axis=0,
        concat_axis=0,
        tiled=True,
    )
    partial_sum = jnp.sum(pieces.astype(jnp.float32), axis=0)
    arrived = lax.all_to_all(
        partial_sum.reshape(row_block, host_count, col_block),
        "hst",
        split_axis=1,
        concat_axis=1,
        tiled=True,
    )
    return jnp.sum(arrived, axis=1)


def adam(grad_total, master, moment_one, moment_two):
    new_one = beta_one * moment_one + (1.0 - beta_one) * grad_total
    new_two = beta_two * moment_two + (1.0 - beta_two) * grad_total * grad_total
    update = new_one / correct_one / (jnp.sqrt(new_two / correct_two) + epsilon)
    new_master = master - learn_rate * (update + decay_rate * master)
    return new_master, new_one, new_two


def local(grads, master, moment_one, moment_two):
    tuned = lax.axis_size("local") == 4 and lax.axis_size("hst") == 8
    gradient = grads[0, 0]
    grad_total = reduce_blocks(gradient) if tuned else reduce_general(gradient)
    first = adam(grad_total, master, moment_one, moment_two)[0].astype(jnp.bfloat16)
    again, first = lax.optimization_barrier((grad_total, first))
    mine = adam(again, master, moment_one, moment_two)[0].astype(jnp.bfloat16)
    if tuned:
        secondary, corner = gather_blocks(first, mine)
    else:
        secondary = corner = lax.all_gather(mine, "hst", axis=1, tiled=True)
    grad_total, _ = lax.optimization_barrier((again, corner))
    new_master, new_one, new_two = adam(grad_total, master, moment_one, moment_two)
    return (grad_total, new_master, new_one, new_two, secondary)


def solution(mesh):
    return jax.shard_map(
        local,
        mesh=mesh,
        in_specs=(
            P("hst", "local", None, None),
            P("local", "hst"),
            P("local", "hst"),
            P("local", "hst"),
        ),
        out_specs=(
            P("local", "hst"),
            P("local", "hst"),
            P("local", "hst"),
            P("local", "hst"),
            P("local", None),
        ),
        check_vma=False,
    )
```

```python
import jax
import jax.numpy as jnp
from jax import lax
from jax.experimental import pallas as pl
from jax.experimental.pallas import tpu as pltpu
from jax.sharding import PartitionSpec as P

beta_one = 0.9
beta_two = 0.95
learn_rate = 0.02
decay_rate = 0.1
epsilon = 1e-08
correct_one = 1.0 - (0.9**50) ** 2
correct_two = 1.0 - (0.95**50) ** 2

wire_scale = 4096.0


def flip_pairs(flips):
    count = lax.axis_size("hst") * lax.axis_size("local")
    return [(i, i ^ flips[i % 2]) for i in range(count)]


def swap(value, *flips):
    return lax.ppermute(value, ("hst", "local"), flip_pairs(flips))


def narrow(value):
    return (value * wire_scale).astype(jnp.float16)


def widen(value):
    return value.astype(jnp.float32) * (1.0 / wire_scale)


def pick(value, index):
    return lax.dynamic_index_in_dim(value, index, 0, keepdims=False)


CORE, X, Y, Z_NEAR, Z_FAR = 1, 2, 4, 8, 16


def place():
    me_local, me_host = lax.axis_index("local"), lax.axis_index("hst")
    return me_local // 2, me_host % 2, me_host // 2, me_local % 2


def rows_of(core, block, i, store):
    tile, half = block.shape[0] // 2, block.shape[1] // 2
    my_x, my_y, my_z, _ = place()
    z, y = i // 2, i % 2
    block = block.astype(jnp.float32)
    for x in (0, 1):
        left, right = block[x * tile : (x + 1) * tile, :half], block[x * tile : (x + 1) * tile, half:]
        rows = [
            jnp.concatenate([left[at : at + tile // 2], right[at : at + tile // 2]], axis=0).astype(jnp.bfloat16)
            for at in (0, tile // 2)
        ]
        step = jnp.where(core == 0, (2 * my_x + my_y) ^ (2 * x + y), my_z ^ z)
        member = jnp.where(core == 0, z, 2 * x + y)
        store(step, member, jnp.where(core == 0, rows[0], rows[1]))


def theirs_kernel(whole, first, others, landed, arrived):
    half = first.shape[2]
    core = place()[3]
    parts = [pl.ds(i * half, half) for i in range(16)]
    copies = [
        pltpu.make_async_copy(whole.at[:, part], landed.at[:, part], arrived.at[i])
        for i, part in enumerate(parts)
    ]
    for copy in copies:
        copy.start()

    def store(step, member, rows):
        @pl.when(step == 3)
        def _():
            first[member] = rows

        @pl.when(step != 3)
        def _():
            others[step, member] = rows

    for i in range(8):
        copies[2 * i].wait()
        copies[2 * i + 1].wait()
        rows_of(1 - core, landed[:, pl.ds(2 * i * half, 2 * half)], i, store)


def own_kernel(landed, own):
    half = own.shape[3]
    core = place()[3]

    def store(step, member, rows):
        own[step, member] = rows

    for i in range(8):
        rows_of(core, landed[:, pl.ds(2 * i * half, 2 * half)], i, store)


def call(kernel, operand, space, outs, scratch=()):
    size = operand.size
    return pl.pallas_call(
        kernel,
        in_specs=[pl.BlockSpec(memory_space=space)],
        out_specs=[pl.BlockSpec(memory_space=pltpu.VMEM)] * len(outs),
        out_shape=[pltpu.VMEM(shape, operand.dtype) for shape in outs],
        scratch_shapes=scratch,
        compiler_params=pltpu.CompilerParams(vmem_limit_bytes=8 << 20),
        cost_estimate=pl.CostEstimate(flops=size, bytes_accessed=4 * size, transcendentals=0),
    )(pltpu.with_memory_space_constraint(operand, space))


def split_rows(gradient):
    rows, cols = gradient.shape
    shape = (4, rows // 2, cols // 16)
    first, others, landed = call(
        theirs_kernel,
        gradient,
        pltpu.HBM,
        [shape, (3, *shape), gradient.shape],
        [pltpu.SemaphoreType.DMA((16,))],
    )
    first, others, landed = lax.optimization_barrier((first, others, landed))
    (own,) = call(own_kernel, landed, pltpu.VMEM, [(4, *shape)])
    return first, others, own


def reduce_blocks(gradient):
    tile = gradient.shape[0] // 2
    x, y, z, core = place()

    first, others, own = split_rows(gradient)
    first, others = swap(first, CORE, CORE), swap(others, CORE, CORE)

    def pair(d):
        return own[d].astype(jnp.float32) + (first if d == 3 else others[d]).astype(jnp.float32)

    over_xy, over_z = (0, Y, X, X + Y), (0, Z_NEAR, Z_FAR, Z_NEAR + Z_FAR)
    sent = {3: narrow(pair(3))}
    own, sent[3] = lax.optimization_barrier((own, sent[3]))
    sent.update({d: narrow(pair(d)) for d in (1, 2)})
    got = [swap(sent[d], over_xy[d], over_z[d]) for d in (3, 1, 2)]
    quarter = lax.optimization_barrier(pair(0) + widen(got[0]))
    quarter = quarter + widen(got[1]) + widen(got[2])
    me = jnp.where(core == 0, z, 2 * x + y)
    got = [swap(narrow(pick(quarter, me ^ d)), over_z[d], over_xy[d]) for d in (1, 2, 3)]
    total = pick(quarter, me) + widen(got[0]) + widen(got[1]) + widen(got[2])

    return jnp.concatenate([total[: tile // 2], total[tile // 2 :]], axis=1)


def gather_blocks(first, mine):
    row_block, col_block = mine.shape
    me = lax.axis_index("hst")
    far = swap(first, Z_FAR, Z_FAR)
    corner, far_corner = (swap(mine, f, f) for f in (Z_NEAR + Y, Z_FAR + Z_NEAR + Y))
    pair = jnp.stack([mine, far])
    near, side = swap(pair, Z_NEAR, Z_NEAR), swap(pair, Y, Y)
    got = [(0, mine), (3, corner), (4, far), (7, far_corner)]
    got += [(2, near[0]), (6, near[1]), (1, side[0]), (5, side[1])]
    whole = jnp.zeros((row_block, 8 * col_block), mine.dtype)
    for bits, block in got:
        whole = lax.dynamic_update_slice_in_dim(whole, block, (me ^ bits) * col_block, 1)
    return whole, corner


def reduce_general(gradient):
    local_count = lax.axis_size("local")
    host_count = lax.axis_size("hst")
    rows, cols = gradient.shape
    row_block, col_block = rows // local_count, cols // host_count
    pieces = lax.all_to_all(
        gradient.reshape(local_count, row_block, cols),
        "local",
        split_axis=0,
        concat_axis=0,
        tiled=True,
    )
    partial_sum = jnp.sum(pieces.astype(jnp.float32), axis=0)
    arrived = lax.all_to_all(
        partial_sum.reshape(row_block, host_count, col_block),
        "hst",
        split_axis=1,
        concat_axis=1,
        tiled=True,
    )
    return jnp.sum(arrived, axis=1)


def adam(grad_total, master, moment_one, moment_two):
    new_one = beta_one * moment_one + (1.0 - beta_one) * grad_total
    new_two = beta_two * moment_two + (1.0 - beta_two) * grad_total * grad_total
    update = new_one / correct_one / (jnp.sqrt(new_two / correct_two) + epsilon)
    new_master = master - learn_rate * (update + decay_rate * master)
    return new_master, new_one, new_two


def local(grads, master, moment_one, moment_two):
    tuned = lax.axis_size("local") == 4 and lax.axis_size("hst") == 8
    gradient = grads[0, 0]
    grad_total = reduce_blocks(gradient) if tuned else reduce_general(gradient)
    first = adam(grad_total, master, moment_one, moment_two)[0].astype(jnp.bfloat16)
    again, first = lax.optimization_barrier((grad_total, first))
    mine = adam(again, master, moment_one, moment_two)[0].astype(jnp.bfloat16)
    if tuned:
        secondary, corner = gather_blocks(first, mine)
    else:
        secondary = corner = lax.all_gather(mine, "hst", axis=1, tiled=True)
    grad_total, _ = lax.optimization_barrier((again, corner))
    new_master, new_one, new_two = adam(grad_total, master, moment_one, moment_two)
    return (grad_total, new_master, new_one, new_two, secondary)


def solution(mesh):
    return jax.shard_map(
        local,
        mesh=mesh,
        in_specs=(
            P("hst", "local", None, None),
            P("local", "hst"),
            P("local", "hst"),
            P("local", "hst"),
        ),
        out_specs=(
            P("local", "hst"),
            P("local", "hst"),
            P("local", "hst"),
            P("local", "hst"),
            P("local", None),
        ),
        check_vma=False,
    )
```

```python
import jax
import jax.numpy as jnp
from jax import lax
from jax.experimental import pallas as pl
from jax.experimental.pallas import tpu as pltpu
from jax.sharding import PartitionSpec as P

beta_one = 0.9
beta_two = 0.95
learn_rate = 0.02
decay_rate = 0.1
epsilon = 1e-08
correct_one = 1.0 - (0.9**50) ** 2
correct_two = 1.0 - (0.95**50) ** 2

wire_scale = 4096.0


def flip_pairs(flips):
    count = lax.axis_size("hst") * lax.axis_size("local")
    return [(i, i ^ flips[i % 2]) for i in range(count)]


def swap(value, *flips):
    return lax.ppermute(value, ("hst", "local"), flip_pairs(flips))


def narrow(value):
    return (value * wire_scale).astype(jnp.float16)


def widen(value):
    return value.astype(jnp.float32) * (1.0 / wire_scale)


def pick(value, index):
    return lax.dynamic_index_in_dim(value, index, 0, keepdims=False)


CORE, X, Y, Z_NEAR, Z_FAR = 1, 2, 4, 8, 16


def place():
    me_local, me_host = lax.axis_index("local"), lax.axis_index("hst")
    return me_local // 2, me_host % 2, me_host // 2, me_local % 2


def rows_of(core, block, i, store):
    tile, half = block.shape[0] // 2, block.shape[1] // 2
    my_x, my_y, my_z, _ = place()
    z, y = i // 2, i % 2
    block = block.astype(jnp.float32)
    for x in (0, 1):
        left, right = block[x * tile : (x + 1) * tile, :half], block[x * tile : (x + 1) * tile, half:]
        rows = [
            jnp.concatenate([left[at : at + tile // 2], right[at : at + tile // 2]], axis=0).astype(jnp.bfloat16)
            for at in (0, tile // 2)
        ]
        step = jnp.where(core == 0, (2 * my_x + my_y) ^ (2 * x + y), my_z ^ z)
        member = jnp.where(core == 0, z, 2 * x + y)
        store(step, member, jnp.where(core == 0, rows[0], rows[1]))


def theirs_kernel(whole, first, others, landed, arrived):
    half = first.shape[2]
    core = place()[3]
    parts = [pl.ds(i * half, half) for i in range(16)]
    copies = [
        pltpu.make_async_copy(whole.at[:, part], landed.at[:, part], arrived.at[i])
        for i, part in enumerate(parts)
    ]
    for copy in copies:
        copy.start()

    def store(step, member, rows):
        @pl.when(step == 3)
        def _():
            first[member] = rows

        @pl.when(step != 3)
        def _():
            others[step, member] = rows

    for i in range(8):
        copies[2 * i].wait()
        copies[2 * i + 1].wait()
        rows_of(1 - core, landed[:, pl.ds(2 * i * half, 2 * half)], i, store)


def own_kernel(landed, own):
    half = own.shape[3]
    core = place()[3]

    def store(step, member, rows):
        own[step, member] = rows

    for i in range(8):
        rows_of(core, landed[:, pl.ds(2 * i * half, 2 * half)], i, store)


def call(kernel, operand, space, outs, scratch=()):
    size = operand.size
    return pl.pallas_call(
        kernel,
        in_specs=[pl.BlockSpec(memory_space=space)],
        out_specs=[pl.BlockSpec(memory_space=pltpu.VMEM)] * len(outs),
        out_shape=[pltpu.VMEM(shape, operand.dtype) for shape in outs],
        scratch_shapes=scratch,
        compiler_params=pltpu.CompilerParams(vmem_limit_bytes=8 << 20),
        cost_estimate=pl.CostEstimate(flops=size, bytes_accessed=4 * size, transcendentals=0),
    )(pltpu.with_memory_space_constraint(operand, space))


def split_rows(gradient):
    rows, cols = gradient.shape
    shape = (4, rows // 2, cols // 16)
    first, others, landed = call(
        theirs_kernel,
        gradient,
        pltpu.HBM,
        [shape, (3, *shape), gradient.shape],
        [pltpu.SemaphoreType.DMA((16,))],
    )
    first, others, landed = lax.optimization_barrier((first, others, landed))
    (own,) = call(own_kernel, landed, pltpu.VMEM, [(4, *shape)])
    return first, others, own


def reduce_blocks(gradient):
    tile = gradient.shape[0] // 2
    x, y, z, core = place()

    first, others, own = split_rows(gradient)
    first, others = swap(first, CORE, CORE), swap(others, CORE, CORE)

    def pair(d):
        return own[d].astype(jnp.float32) + (first if d == 3 else others[d]).astype(jnp.float32)

    over_xy, over_z = (0, Y, X, X + Y), (0, Z_NEAR, Z_FAR, Z_NEAR + Z_FAR)
    sent = {3: narrow(pair(3))}
    own, sent[3] = lax.optimization_barrier((own, sent[3]))
    sent.update({d: narrow(pair(d)) for d in (1, 2)})
    got = [swap(sent[d], over_xy[d], over_z[d]) for d in (3, 1, 2)]
    quarter = lax.optimization_barrier(pair(0) + widen(got[0]))
    quarter = quarter + widen(got[1]) + widen(got[2])
    me = jnp.where(core == 0, z, 2 * x + y)
    got = [swap(narrow(pick(quarter, me ^ d)), over_z[d], over_xy[d]) for d in (1, 2, 3)]
    total = pick(quarter, me) + widen(got[0]) + widen(got[1]) + widen(got[2])

    return jnp.concatenate([total[: tile // 2], total[tile // 2 :]], axis=1)


def gather_blocks(first, mine):
    row_block, col_block = mine.shape
    me, core = lax.axis_index("hst"), place()[3]
    far = swap(first, Z_FAR, Z_FAR)
    corner, cross = swap(mine, Z_NEAR + Y, Z_FAR + Z_NEAR + Y), swap(mine, Z_FAR + Z_NEAR + Y, Z_NEAR + Y)
    pair = jnp.stack([mine, far])
    side, other_side = swap(pair, Z_NEAR, Y), swap(pair, Y, Z_NEAR)
    bits = lambda at_0, at_1: jnp.where(core == 0, at_0, at_1)
    got = [(0, mine), (4, far), (bits(3, 7), corner), (bits(7, 3), cross)]
    got += [(bits(2, 1) + 4 * i, side[i]) for i in (0, 1)]
    got += [(bits(1, 2) + 4 * i, other_side[i]) for i in (0, 1)]
    whole = jnp.zeros((row_block, 8 * col_block), mine.dtype)
    for away, block in got:
        whole = lax.dynamic_update_slice_in_dim(whole, block, (me ^ away) * col_block, 1)
    return whole, corner


def reduce_general(gradient):
    local_count = lax.axis_size("local")
    host_count = lax.axis_size("hst")
    rows, cols = gradient.shape
    row_block, col_block = rows // local_count, cols // host_count
    pieces = lax.all_to_all(
        gradient.reshape(local_count, row_block, cols),
        "local",
        split_axis=0,
        concat_axis=0,
        tiled=True,
    )
    partial_sum = jnp.sum(pieces.astype(jnp.float32), axis=0)
    arrived = lax.all_to_all(
        partial_sum.reshape(row_block, host_count, col_block),
        "hst",
        split_axis=1,
        concat_axis=1,
        tiled=True,
    )
    return jnp.sum(arrived, axis=1)


def adam(grad_total, master, moment_one, moment_two):
    new_one = beta_one * moment_one + (1.0 - beta_one) * grad_total
    new_two = beta_two * moment_two + (1.0 - beta_two) * grad_total * grad_total
    update = new_one / correct_one / (jnp.sqrt(new_two / correct_two) + epsilon)
    new_master = master - learn_rate * (update + decay_rate * master)
    return new_master, new_one, new_two


def local(grads, master, moment_one, moment_two):
    tuned = lax.axis_size("local") == 4 and lax.axis_size("hst") == 8
    gradient = grads[0, 0]
    grad_total = reduce_blocks(gradient) if tuned else reduce_general(gradient)
    first = adam(grad_total, master, moment_one, moment_two)[0].astype(jnp.bfloat16)
    again, first = lax.optimization_barrier((grad_total, first))
    mine = adam(again, master, moment_one, moment_two)[0].astype(jnp.bfloat16)
    if tuned:
        secondary, corner = gather_blocks(first, mine)
    else:
        secondary = corner = lax.all_gather(mine, "hst", axis=1, tiled=True)
    grad_total, _ = lax.optimization_barrier((again, corner))
    new_master, new_one, new_two = adam(grad_total, master, moment_one, moment_two)
    return (grad_total, new_master, new_one, new_two, secondary)


def solution(mesh):
    return jax.shard_map(
        local,
        mesh=mesh,
        in_specs=(
            P("hst", "local", None, None),
            P("local", "hst"),
            P("local", "hst"),
            P("local", "hst"),
        ),
        out_specs=(
            P("local", "hst"),
            P("local", "hst"),
            P("local", "hst"),
            P("local", "hst"),
            P("local", None),
        ),
        check_vma=False,
    )
```

```python
import jax
import jax.numpy as jnp
from jax import lax
from jax.experimental import pallas as pl
from jax.experimental.pallas import tpu as pltpu
from jax.sharding import PartitionSpec as P

beta_one = 0.9
beta_two = 0.95
learn_rate = 0.02
decay_rate = 0.1
epsilon = 1e-08
correct_one = 1.0 - (0.9**50) ** 2
correct_two = 1.0 - (0.95**50) ** 2

wire_scale = 4096.0


def flip_pairs(flips):
    count = lax.axis_size("hst") * lax.axis_size("local")
    return [(i, i ^ flips[i % 2]) for i in range(count)]


def swap(value, *flips):
    return lax.ppermute(value, ("hst", "local"), flip_pairs(flips))


def narrow(value):
    return (value * wire_scale).astype(jnp.float16)


def widen(value):
    return value.astype(jnp.float32) * (1.0 / wire_scale)


def pick(value, index):
    return lax.dynamic_index_in_dim(value, index, 0, keepdims=False)


CORE, X, Y, Z_NEAR, Z_FAR = 1, 2, 4, 8, 16


def place():
    me_local, me_host = lax.axis_index("local"), lax.axis_index("hst")
    return me_local // 2, me_host % 2, me_host // 2, me_local % 2


def tiles_of(block):
    tile, half = block.shape[0] // 2, block.shape[1] // 2
    block = block.astype(jnp.float32)
    found = []
    for x in (0, 1):
        left, right = block[x * tile : (x + 1) * tile, :half], block[x * tile : (x + 1) * tile, half:]
        found.append(
            [
                jnp.concatenate([left[at : at + tile // 2], right[at : at + tile // 2]], axis=0).astype(jnp.bfloat16)
                for at in (0, tile // 2)
            ]
        )
    return found


def order():
    _, y, z, _ = place()
    far_z, far_y = z ^ 3, 1 - y
    return [(far_z, far_y), (far_z, y)] + [(far_z ^ k, at) for at in (far_y, y) for k in (1, 2, 3)]


def fetch(whole, landed, arrived, blocks):
    cols = landed.shape[2]
    copies = []
    for i, (z, y) in enumerate(blocks):
        at = pl.multiple_of((2 * z + y) * cols, 128)
        copies.append(pltpu.make_async_copy(whole.at[:, pl.ds(at, cols)], landed.at[i], arrived.at[i]))
        copies[-1].start()
    return copies


def far_kernel(whole, theirs, own, landed, arrived):
    my_x, _, _, core = place()
    blocks = order()[:5]
    copies = fetch(whole, landed, arrived, blocks)

    def store(of_core, member, rows):
        @pl.when(core == of_core)
        def _():
            own[member] = rows

        @pl.when(core != of_core)
        def _():
            theirs[member] = rows

    for i, (z, y) in enumerate(blocks):
        copies[i].wait()
        tiles = tiles_of(landed[i])
        if i < 2:
            for x in (0, 1):
                store(1, 2 * x + y, tiles[x][1])
        if i != 1:
            store(0, z, jnp.where(my_x == 0, tiles[1][0], tiles[0][0]))


def store_rest(core, block, z, y, out):
    my_x, my_y, my_z, _ = place()
    tiles = tiles_of(block)
    for x in (0, 1):
        step = jnp.where(core == 0, (2 * my_x + my_y) ^ (2 * x + y), my_z ^ z)
        member = jnp.where(core == 0, z, 2 * x + y)

        @pl.when(step != 3)
        def _(x=x, step=step, member=member):
            out[step, member] = jnp.where(core == 0, tiles[x][0], tiles[x][1])


def theirs_kernel(whole, landed, out, landed_rest, arrived):
    core, blocks = place()[3], order()
    copies = fetch(whole, landed_rest, arrived, blocks[5:])
    for i, (z, y) in enumerate(blocks):
        if i >= 5:
            copies[i - 5].wait()
        store_rest(1 - core, landed[i] if i < 5 else landed_rest[i - 5], z, y, out)


def own_kernel(landed, landed_rest, out):
    core = place()[3]
    for i, (z, y) in enumerate(order()):
        store_rest(core, landed[i] if i < 5 else landed_rest[i - 5], z, y, out)


def call(kernel, operands, outs, copies=0):
    spaces = [pltpu.HBM if copies and i == 0 else pltpu.VMEM for i in range(len(operands))]
    size = operands[0].size
    return pl.pallas_call(
        kernel,
        in_specs=[pl.BlockSpec(memory_space=space) for space in spaces],
        out_specs=[pl.BlockSpec(memory_space=pltpu.VMEM)] * len(outs),
        out_shape=[pltpu.VMEM(shape, jnp.bfloat16) for shape in outs],
        scratch_shapes=[pltpu.SemaphoreType.DMA((copies,))] if copies else [],
        compiler_params=pltpu.CompilerParams(vmem_limit_bytes=8 << 20),
        cost_estimate=pl.CostEstimate(flops=size, bytes_accessed=4 * size, transcendentals=0),
    )(*[pltpu.with_memory_space_constraint(v, space) for v, space in zip(operands, spaces)])


def split_rows(gradient):
    rows, cols = gradient.shape
    shape, block = (4, rows // 2, cols // 16), (rows, cols // 8)
    theirs, own, landed = call(far_kernel, [gradient], [shape, shape, (5, *block)], copies=5)
    theirs, landed = lax.optimization_barrier((theirs, landed))
    theirs_rest, landed_rest = call(theirs_kernel, [gradient, landed], [(3, *shape), (3, *block)], copies=3)
    return theirs, own, theirs_rest, [landed, landed_rest]


def reduce_blocks(gradient):
    tile = gradient.shape[0] // 2
    x, y, z, core = place()

    theirs, own, theirs_rest, landed = split_rows(gradient)
    other, other_rest = swap(theirs, CORE, CORE), swap(theirs_rest, CORE, CORE)

    over_xy, over_z = (0, Y, X, X + Y), (0, Z_NEAR, Z_FAR, Z_NEAR + Z_FAR)
    sent = {3: narrow(own.astype(jnp.float32) + other.astype(jnp.float32))}
    *landed, sent[3] = lax.optimization_barrier((*landed, sent[3]))
    (own_rest,) = call(own_kernel, landed, [(3, *own.shape)])

    def pair(d):
        return own_rest[d].astype(jnp.float32) + other_rest[d].astype(jnp.float32)

    sent.update({d: narrow(pair(d)) for d in (1, 2)})
    got = [swap(sent[d], over_xy[d], over_z[d]) for d in (3, 2, 1)]
    quarter = lax.optimization_barrier(pair(0) + widen(got[0]))
    quarter = quarter + widen(got[1]) + widen(got[2])
    me = jnp.where(core == 0, z, 2 * x + y)
    got = [swap(narrow(pick(quarter, me ^ d)), over_z[d], over_xy[d]) for d in (3, 2, 1)]
    total = pick(quarter, me) + widen(got[0]) + widen(got[1]) + widen(got[2])

    return jnp.concatenate([total[: tile // 2], total[tile // 2 :]], axis=1)


def gather_blocks(first, mine):
    row_block, col_block = mine.shape
    me, core = lax.axis_index("hst"), place()[3]
    far = swap(first, Z_FAR, Z_FAR)
    corner, cross = swap(mine, Z_NEAR + Y, Z_FAR + Z_NEAR + Y), swap(mine, Z_FAR + Z_NEAR + Y, Z_NEAR + Y)
    pair = jnp.stack([mine, far])
    side, other_side = swap(pair, Z_NEAR, Y), swap(pair, Y, Z_NEAR)
    bits = lambda at_0, at_1: jnp.where(core == 0, at_0, at_1)
    got = [(0, mine), (4, far), (bits(3, 7), corner), (bits(7, 3), cross)]
    got += [(bits(2, 1) + 4 * i, side[i]) for i in (0, 1)]
    got += [(bits(1, 2) + 4 * i, other_side[i]) for i in (0, 1)]
    whole = jnp.zeros((row_block, 8 * col_block), mine.dtype)
    for away, block in got:
        whole = lax.dynamic_update_slice_in_dim(whole, block, (me ^ away) * col_block, 1)
    return whole, corner


def reduce_general(gradient):
    local_count = lax.axis_size("local")
    host_count = lax.axis_size("hst")
    rows, cols = gradient.shape
    row_block, col_block = rows // local_count, cols // host_count
    pieces = lax.all_to_all(
        gradient.reshape(local_count, row_block, cols),
        "local",
        split_axis=0,
        concat_axis=0,
        tiled=True,
    )
    partial_sum = jnp.sum(pieces.astype(jnp.float32), axis=0)
    arrived = lax.all_to_all(
        partial_sum.reshape(row_block, host_count, col_block),
        "hst",
        split_axis=1,
        concat_axis=1,
        tiled=True,
    )
    return jnp.sum(arrived, axis=1)


def adam(grad_total, master, moment_one, moment_two):
    new_one = beta_one * moment_one + (1.0 - beta_one) * grad_total
    new_two = beta_two * moment_two + (1.0 - beta_two) * grad_total * grad_total
    update = new_one / correct_one / (jnp.sqrt(new_two / correct_two) + epsilon)
    new_master = master - learn_rate * (update + decay_rate * master)
    return new_master, new_one, new_two


def local(grads, master, moment_one, moment_two):
    tuned = lax.axis_size("local") == 4 and lax.axis_size("hst") == 8
    gradient = grads[0, 0]
    grad_total = reduce_blocks(gradient) if tuned else reduce_general(gradient)
    first = adam(grad_total, master, moment_one, moment_two)[0].astype(jnp.bfloat16)
    again, first = lax.optimization_barrier((grad_total, first))
    mine = adam(again, master, moment_one, moment_two)[0].astype(jnp.bfloat16)
    if tuned:
        secondary, corner = gather_blocks(first, mine)
    else:
        secondary = corner = lax.all_gather(mine, "hst", axis=1, tiled=True)
    grad_total, _ = lax.optimization_barrier((again, corner))
    new_master, new_one, new_two = adam(grad_total, master, moment_one, moment_two)
    return (grad_total, new_master, new_one, new_two, secondary)


def solution(mesh):
    return jax.shard_map(
        local,
        mesh=mesh,
        in_specs=(
            P("hst", "local", None, None),
            P("local", "hst"),
            P("local", "hst"),
            P("local", "hst"),
        ),
        out_specs=(
            P("local", "hst"),
            P("local", "hst"),
            P("local", "hst"),
            P("local", "hst"),
            P("local", None),
        ),
        check_vma=False,
    )
```

```python
import jax
import jax.numpy as jnp
from jax import lax
from jax.experimental import pallas as pl
from jax.experimental.pallas import tpu as pltpu
from jax.sharding import PartitionSpec as P

beta_one = 0.9
beta_two = 0.95
learn_rate = 0.02
decay_rate = 0.1
epsilon = 1e-08
correct_one = 1.0 - (0.9**50) ** 2
correct_two = 1.0 - (0.95**50) ** 2

wire_scale = 4096.0


def flip_pairs(flips):
    count = lax.axis_size("hst") * lax.axis_size("local")
    return [(i, i ^ flips[i % 2]) for i in range(count)]


def swap(value, *flips):
    return lax.ppermute(value, ("hst", "local"), flip_pairs(flips))


def narrow(value):
    return (value * wire_scale).astype(jnp.float16)


def widen(value):
    return value.astype(jnp.float32) * (1.0 / wire_scale)


def pick(value, index):
    return lax.dynamic_index_in_dim(value, index, 0, keepdims=False)


CORE, X, Y, Z_NEAR, Z_FAR = 1, 2, 4, 8, 16


def place():
    me_local, me_host = lax.axis_index("local"), lax.axis_index("hst")
    return me_local // 2, me_host % 2, me_host // 2, me_local % 2


def rows_of(core, block, i, store):
    tile, half = block.shape[0] // 2, block.shape[1] // 2
    my_x, my_y, my_z, _ = place()
    z, y = i // 2, i % 2
    block = block.astype(jnp.float32)
    for x in (0, 1):
        left, right = block[x * tile : (x + 1) * tile, :half], block[x * tile : (x + 1) * tile, half:]
        rows = [
            jnp.concatenate([left[at : at + tile // 2], right[at : at + tile // 2]], axis=0).astype(jnp.bfloat16)
            for at in (0, tile // 2)
        ]
        step = jnp.where(core == 0, (2 * my_x + my_y) ^ (2 * x + y), my_z ^ z)
        member = jnp.where(core == 0, z, 2 * x + y)
        store(step, member, jnp.where(core == 0, rows[0], rows[1]))


def theirs_kernel(whole, first, others, landed, arrived):
    half = first.shape[2]
    core = place()[3]
    parts = [pl.ds(i * half, half) for i in range(16)]
    copies = [
        pltpu.make_async_copy(whole.at[:, part], landed.at[:, part], arrived.at[i])
        for i, part in enumerate(parts)
    ]
    for copy in copies:
        copy.start()

    def store(step, member, rows):
        @pl.when(step == 3)
        def _():
            first[member] = rows

        @pl.when(step != 3)
        def _():
            others[step, member] = rows

    for i in range(8):
        copies[2 * i].wait()
        copies[2 * i + 1].wait()
        rows_of(1 - core, landed[:, pl.ds(2 * i * half, 2 * half)], i, store)


def own_kernel(landed, own):
    half = own.shape[3]
    core = place()[3]

    def store(step, member, rows):
        own[step, member] = rows

    for i in range(8):
        rows_of(core, landed[:, pl.ds(2 * i * half, 2 * half)], i, store)


def call(kernel, operand, space, outs, scratch=()):
    size = operand.size
    return pl.pallas_call(
        kernel,
        in_specs=[pl.BlockSpec(memory_space=space)],
        out_specs=[pl.BlockSpec(memory_space=pltpu.VMEM)] * len(outs),
        out_shape=[pltpu.VMEM(shape, operand.dtype) for shape in outs],
        scratch_shapes=scratch,
        compiler_params=pltpu.CompilerParams(vmem_limit_bytes=8 << 20),
        cost_estimate=pl.CostEstimate(flops=size, bytes_accessed=4 * size, transcendentals=0),
    )(pltpu.with_memory_space_constraint(operand, space))


def split_rows(gradient):
    rows, cols = gradient.shape
    shape = (4, rows // 2, cols // 16)
    first, others, landed = call(
        theirs_kernel,
        gradient,
        pltpu.HBM,
        [shape, (3, *shape), gradient.shape],
        [pltpu.SemaphoreType.DMA((16,))],
    )
    first, others, landed = lax.optimization_barrier((first, others, landed))
    (own,) = call(own_kernel, landed, pltpu.VMEM, [(4, *shape)])
    return first, others, own


def reduce_blocks(gradient):
    tile = gradient.shape[0] // 2
    x, y, z, core = place()

    first, others, own = split_rows(gradient)
    first, others = swap(first, CORE, CORE), swap(others, CORE, CORE)

    def pair(d):
        return own[d].astype(jnp.float32) + (first if d == 3 else others[d]).astype(jnp.float32)

    over_xy, over_z = (0, Y, X, X + Y), (0, Z_NEAR, Z_FAR, Z_NEAR + Z_FAR)
    sent = {3: narrow(pair(3))}
    own, sent[3] = lax.optimization_barrier((own, sent[3]))
    sent.update({d: narrow(pair(d)) for d in (1, 2)})
    got = [swap(sent[d], over_xy[d], over_z[d]) for d in (3, 1, 2)]
    quarter = lax.optimization_barrier(pair(0) + widen(got[0]))
    quarter = quarter + widen(got[1]) + widen(got[2])
    me = jnp.where(core == 0, z, 2 * x + y)
    got = [swap(narrow(pick(quarter, me ^ d)), over_z[d], over_xy[d]) for d in (1, 2, 3)]
    total = pick(quarter, me) + widen(got[0]) + widen(got[1]) + widen(got[2])

    return jnp.concatenate([total[: tile // 2], total[tile // 2 :]], axis=1)


def gather_blocks(mine):
    row_block, col_block = mine.shape
    me, core = lax.axis_index("hst"), place()[3]
    pair = jnp.stack(lax.optimization_barrier([mine, swap(mine, Z_FAR, Z_FAR)]))
    got = [pair] + [swap(pair, *f) for f in ((Z_NEAR + Y, Z_NEAR + Y), (Z_NEAR, Y), (Y, Z_NEAR))]
    away = [0, 3, jnp.where(core == 0, 2, 1), jnp.where(core == 0, 1, 2)]
    whole = jnp.zeros((row_block, 8 * col_block), mine.dtype)
    for bits, blocks in zip(away, got):
        for i in (0, 1):
            place_at = (me ^ bits ^ (4 * i)) * col_block
            whole = lax.dynamic_update_slice_in_dim(whole, blocks[i], place_at, 1)
    return whole


def reduce_general(gradient):
    local_count = lax.axis_size("local")
    host_count = lax.axis_size("hst")
    rows, cols = gradient.shape
    row_block, col_block = rows // local_count, cols // host_count
    pieces = lax.all_to_all(
        gradient.reshape(local_count, row_block, cols),
        "local",
        split_axis=0,
        concat_axis=0,
        tiled=True,
    )
    partial_sum = jnp.sum(pieces.astype(jnp.float32), axis=0)
    arrived = lax.all_to_all(
        partial_sum.reshape(row_block, host_count, col_block),
        "hst",
        split_axis=1,
        concat_axis=1,
        tiled=True,
    )
    return jnp.sum(arrived, axis=1)


def adam(grad_total, master, moment_one, moment_two):
    new_one = beta_one * moment_one + (1.0 - beta_one) * grad_total
    new_two = beta_two * moment_two + (1.0 - beta_two) * grad_total * grad_total
    update = new_one / correct_one / (jnp.sqrt(new_two / correct_two) + epsilon)
    new_master = master - learn_rate * (update + decay_rate * master)
    return new_master, new_one, new_two


def local(grads, master, moment_one, moment_two):
    tuned = lax.axis_size("local") == 4 and lax.axis_size("hst") == 8
    gradient = grads[0, 0]
    grad_total = reduce_blocks(gradient) if tuned else reduce_general(gradient)
    mine = adam(grad_total, master, moment_one, moment_two)[0].astype(jnp.bfloat16)
    if tuned:
        secondary = gather_blocks(mine)
    else:
        secondary = lax.all_gather(mine, "hst", axis=1, tiled=True)
    grad_total, _ = lax.optimization_barrier((grad_total, mine))
    new_master, new_one, new_two = adam(grad_total, master, moment_one, moment_two)
    return (grad_total, new_master, new_one, new_two, secondary)


def solution(mesh):
    return jax.shard_map(
        local,
        mesh=mesh,
        in_specs=(
            P("hst", "local", None, None),
            P("local", "hst"),
            P("local", "hst"),
            P("local", "hst"),
        ),
        out_specs=(
            P("local", "hst"),
            P("local", "hst"),
            P("local", "hst"),
            P("local", "hst"),
            P("local", None),
        ),
        check_vma=False,
    )
```

```python
import jax
import jax.numpy as jnp
from jax import lax
from jax.experimental import pallas as pl
from jax.experimental.pallas import tpu as pltpu
from jax.sharding import PartitionSpec as P

beta_one = 0.9
beta_two = 0.95
learn_rate = 0.02
decay_rate = 0.1
epsilon = 1e-08
correct_one = 1.0 - (0.9**50) ** 2
correct_two = 1.0 - (0.95**50) ** 2

wire_scale = 4096.0


def flip_pairs(flips):
    count = lax.axis_size("hst") * lax.axis_size("local")
    return [(i, i ^ flips[i % 2]) for i in range(count)]


def swap(value, *flips):
    return lax.ppermute(value, ("hst", "local"), flip_pairs(flips))


def narrow(value):
    return (value * wire_scale).astype(jnp.float16)


def widen(value):
    return value.astype(jnp.float32) * (1.0 / wire_scale)


def pick(value, index):
    return lax.dynamic_index_in_dim(value, index, 0, keepdims=False)


CORE, X, Y, Z_NEAR, Z_FAR = 1, 2, 4, 8, 16


def place():
    me_local, me_host = lax.axis_index("local"), lax.axis_index("hst")
    return me_local // 2, me_host % 2, me_host // 2, me_local % 2


def rows_of(core, block, i, store):
    tile, half = block.shape[0] // 2, block.shape[1] // 2
    my_x, my_y, my_z, _ = place()
    z, y = i // 2, i % 2
    block = block.astype(jnp.float32)
    for x in (0, 1):
        left, right = block[x * tile : (x + 1) * tile, :half], block[x * tile : (x + 1) * tile, half:]
        rows = [
            jnp.concatenate([left[at : at + tile // 2], right[at : at + tile // 2]], axis=0).astype(jnp.bfloat16)
            for at in (0, tile // 2)
        ]
        step = jnp.where(core == 0, (2 * my_x + my_y) ^ (2 * x + y), my_z ^ z)
        member = jnp.where(core == 0, z, 2 * x + y)
        store(step, member, jnp.where(core == 0, rows[0], rows[1]))


def theirs_kernel(whole, first, others, landed, arrived):
    half = first.shape[2]
    core = place()[3]
    parts = [pl.ds(2 * i * half, 2 * half) for i in range(8)]
    copies = [
        pltpu.make_async_copy(whole.at[:, part], landed.at[:, part], arrived.at[i])
        for i, part in enumerate(parts)
    ]
    for copy in copies:
        copy.start()

    def store(step, member, rows):
        @pl.when(step == 3)
        def _():
            first[member] = rows

        @pl.when(step != 3)
        def _():
            others[step, member] = rows

    for i in range(8):
        copies[i].wait()
        rows_of(1 - core, landed[:, parts[i]], i, store)


def own_kernel(landed, own):
    half = own.shape[3]
    core = place()[3]

    def store(step, member, rows):
        own[step, member] = rows

    for i in range(8):
        rows_of(core, landed[:, pl.ds(2 * i * half, 2 * half)], i, store)


def call(kernel, operand, space, outs, scratch=()):
    size = operand.size
    return pl.pallas_call(
        kernel,
        in_specs=[pl.BlockSpec(memory_space=space)],
        out_specs=[pl.BlockSpec(memory_space=pltpu.VMEM)] * len(outs),
        out_shape=[pltpu.VMEM(shape, operand.dtype) for shape in outs],
        scratch_shapes=scratch,
        compiler_params=pltpu.CompilerParams(vmem_limit_bytes=8 << 20),
        cost_estimate=pl.CostEstimate(flops=size, bytes_accessed=4 * size, transcendentals=0),
    )(pltpu.with_memory_space_constraint(operand, space))


def split_rows(gradient):
    rows, cols = gradient.shape
    shape = (4, rows // 2, cols // 16)
    first, others, landed = call(
        theirs_kernel,
        gradient,
        pltpu.HBM,
        [shape, (3, *shape), gradient.shape],
        [pltpu.SemaphoreType.DMA((8,))],
    )
    first, others, landed = lax.optimization_barrier((first, others, landed))
    (own,) = call(own_kernel, landed, pltpu.VMEM, [(4, *shape)])
    return first, others, own


def reduce_blocks(gradient):
    tile = gradient.shape[0] // 2
    x, y, z, core = place()

    first, others, own = split_rows(gradient)
    first, others = swap(first, CORE, CORE), swap(others, CORE, CORE)

    def pair(d):
        return own[d].astype(jnp.float32) + (first if d == 3 else others[d]).astype(jnp.float32)

    over_xy, over_z = (0, Y, X, X + Y), (0, Z_NEAR, Z_FAR, Z_NEAR + Z_FAR)
    sent = {3: narrow(pair(3))}
    own, sent[3] = lax.optimization_barrier((own, sent[3]))
    sent.update({d: narrow(pair(d)) for d in (1, 2)})
    got = [swap(sent[d], over_xy[d], over_z[d]) for d in (3, 1, 2)]
    quarter = lax.optimization_barrier(pair(0) + widen(got[0]))
    quarter = quarter + widen(got[1]) + widen(got[2])
    me = jnp.where(core == 0, z, 2 * x + y)
    got = [swap(narrow(pick(quarter, me ^ d)), over_z[d], over_xy[d]) for d in (1, 2, 3)]
    total = pick(quarter, me) + widen(got[0]) + widen(got[1]) + widen(got[2])

    return jnp.concatenate([total[: tile // 2], total[tile // 2 :]], axis=1)


def join_kernel(mine, far, corner, cross, side, other_side, whole, left):
    cols = mine.shape[1]
    me, core = lax.axis_index("hst"), place()[3]
    bits = lambda at_0, at_1: jnp.where(core == 0, at_0, at_1)
    pieces = [(0, mine), (4, far), (bits(3, 7), corner), (bits(7, 3), cross)]
    pieces += [(bits(2, 1) + 4 * i, side.at[i]) for i in (0, 1)]
    pieces += [(bits(1, 2) + 4 * i, other_side.at[i]) for i in (0, 1)]
    copies = []
    for i, (away, block) in enumerate(pieces):
        at = pl.multiple_of((me ^ away) * cols, 128)
        copies.append(pltpu.make_async_copy(block, whole.at[:, pl.ds(at, cols)], left.at[i]))
        copies[-1].start()
    for copy in copies:
        copy.wait()


def gather_blocks(first, mine):
    row_block, col_block = mine.shape
    far = swap(first, Z_FAR, Z_FAR)
    corner, cross = swap(mine, Z_NEAR + Y, Z_FAR + Z_NEAR + Y), swap(mine, Z_FAR + Z_NEAR + Y, Z_NEAR + Y)
    pair = jnp.stack([mine, far])
    side, other_side = swap(pair, Z_NEAR, Y), swap(pair, Y, Z_NEAR)
    whole = pl.pallas_call(
        join_kernel,
        in_specs=[pl.BlockSpec(memory_space=pl.ANY)] * 6,
        out_specs=pl.BlockSpec(memory_space=pl.ANY),
        out_shape=jax.ShapeDtypeStruct((row_block, 8 * col_block), mine.dtype),
        scratch_shapes=[pltpu.SemaphoreType.DMA((8,))],
        compiler_params=pltpu.CompilerParams(vmem_limit_bytes=8 << 20),
        cost_estimate=pl.CostEstimate(flops=0, bytes_accessed=4 * 8 * mine.size, transcendentals=0),
    )(mine, far, corner, cross, side, other_side)
    return whole, corner


def reduce_general(gradient):
    local_count = lax.axis_size("local")
    host_count = lax.axis_size("hst")
    rows, cols = gradient.shape
    row_block, col_block = rows // local_count, cols // host_count
    pieces = lax.all_to_all(
        gradient.reshape(local_count, row_block, cols),
        "local",
        split_axis=0,
        concat_axis=0,
        tiled=True,
    )
    partial_sum = jnp.sum(pieces.astype(jnp.float32), axis=0)
    arrived = lax.all_to_all(
        partial_sum.reshape(row_block, host_count, col_block),
        "hst",
        split_axis=1,
        concat_axis=1,
        tiled=True,
    )
    return jnp.sum(arrived, axis=1)


def adam(grad_total, master, moment_one, moment_two):
    new_one = beta_one * moment_one + (1.0 - beta_one) * grad_total
    new_two = beta_two * moment_two + (1.0 - beta_two) * grad_total * grad_total
    update = new_one / correct_one / (jnp.sqrt(new_two / correct_two) + epsilon)
    new_master = master - learn_rate * (update + decay_rate * master)
    return new_master, new_one, new_two


def local(grads, master, moment_one, moment_two):
    tuned = lax.axis_size("local") == 4 and lax.axis_size("hst") == 8
    gradient = grads[0, 0]
    grad_total = reduce_blocks(gradient) if tuned else reduce_general(gradient)
    first = adam(grad_total, master, moment_one, moment_two)[0].astype(jnp.bfloat16)
    again, first = lax.optimization_barrier((grad_total, first))
    mine = adam(again, master, moment_one, moment_two)[0].astype(jnp.bfloat16)
    if tuned:
        secondary, corner = gather_blocks(first, mine)
    else:
        secondary = corner = lax.all_gather(mine, "hst", axis=1, tiled=True)
    grad_total, _ = lax.optimization_barrier((again, corner))
    new_master, new_one, new_two = adam(grad_total, master, moment_one, moment_two)
    return (grad_total, new_master, new_one, new_two, secondary)


def solution(mesh):
    return jax.shard_map(
        local,
        mesh=mesh,
        in_specs=(
            P("hst", "local", None, None),
            P("local", "hst"),
            P("local", "hst"),
            P("local", "hst"),
        ),
        out_specs=(
            P("local", "hst"),
            P("local", "hst"),
            P("local", "hst"),
            P("local", "hst"),
            P("local", None),
        ),
        check_vma=False,
    )
```

```python
import jax
import jax.numpy as jnp
from jax import lax
from jax.experimental import pallas as pl
from jax.experimental.pallas import tpu as pltpu
from jax.sharding import PartitionSpec as P

beta_one = 0.9
beta_two = 0.95
learn_rate = 0.02
decay_rate = 0.1
epsilon = 1e-08
correct_one = 1.0 - (0.9**50) ** 2
correct_two = 1.0 - (0.95**50) ** 2

wire_scale = 4096.0


def flip_pairs(flips):
    count = lax.axis_size("hst") * lax.axis_size("local")
    return [(i, i ^ flips[i % 2]) for i in range(count)]


def swap(value, *flips):
    return lax.ppermute(value, ("hst", "local"), flip_pairs(flips))


def narrow(value):
    return (value * wire_scale).astype(jnp.float16)


def widen(value):
    return value.astype(jnp.float32) * (1.0 / wire_scale)


def pick(value, index):
    return lax.dynamic_index_in_dim(value, index, 0, keepdims=False)


CORE, X, Y, Z_NEAR, Z_FAR = 1, 2, 4, 8, 16


def place():
    me_local, me_host = lax.axis_index("local"), lax.axis_index("hst")
    return me_local // 2, me_host % 2, me_host // 2, me_local % 2


def rows_of(core, block, i, store):
    tile, half = block.shape[0] // 2, block.shape[1] // 2
    my_x, my_y, my_z, _ = place()
    z, y = i // 2, i % 2
    block = block.astype(jnp.float32)
    for x in (0, 1):
        left, right = block[x * tile : (x + 1) * tile, :half], block[x * tile : (x + 1) * tile, half:]
        rows = [
            jnp.concatenate([left[at : at + tile // 2], right[at : at + tile // 2]], axis=0).astype(jnp.bfloat16)
            for at in (0, tile // 2)
        ]
        step = jnp.where(core == 0, (2 * my_x + my_y) ^ (2 * x + y), my_z ^ z)
        member = jnp.where(core == 0, z, 2 * x + y)
        store(step, member, jnp.where(core == 0, rows[0], rows[1]))


def theirs_kernel(whole, first, others, landed, arrived):
    half = first.shape[2]
    core = place()[3]
    parts = [pl.ds(2 * i * half, 2 * half) for i in range(8)]
    copies = [
        pltpu.make_async_copy(whole.at[:, part], landed.at[:, part], arrived.at[i])
        for i, part in enumerate(parts)
    ]
    for copy in copies:
        copy.start()

    def store(step, member, rows):
        @pl.when(step == 2)
        def _():
            first[member] = rows

        @pl.when(step != 2)
        def _():
            others[jnp.minimum(step, 2), member] = rows

    for i in range(8):
        copies[i].wait()
        rows_of(1 - core, landed[:, parts[i]], i, store)


def own_kernel(landed, own):
    half = own.shape[3]
    core = place()[3]

    def store(step, member, rows):
        own[step, member] = rows

    for i in range(8):
        rows_of(core, landed[:, pl.ds(2 * i * half, 2 * half)], i, store)


def call(kernel, operand, space, outs, scratch=()):
    size = operand.size
    return pl.pallas_call(
        kernel,
        in_specs=[pl.BlockSpec(memory_space=space)],
        out_specs=[pl.BlockSpec(memory_space=pltpu.VMEM)] * len(outs),
        out_shape=[pltpu.VMEM(shape, operand.dtype) for shape in outs],
        scratch_shapes=scratch,
        compiler_params=pltpu.CompilerParams(vmem_limit_bytes=8 << 20),
        cost_estimate=pl.CostEstimate(flops=size, bytes_accessed=4 * size, transcendentals=0),
    )(pltpu.with_memory_space_constraint(operand, space))


def split_rows(gradient):
    rows, cols = gradient.shape
    shape = (4, rows // 2, cols // 16)
    first, others, landed = call(
        theirs_kernel,
        gradient,
        pltpu.HBM,
        [shape, (3, *shape), gradient.shape],
        [pltpu.SemaphoreType.DMA((8,))],
    )
    first, others, landed = lax.optimization_barrier((first, others, landed))
    (own,) = call(own_kernel, landed, pltpu.VMEM, [(4, *shape)])
    return first, others, own


def reduce_blocks(gradient):
    tile = gradient.shape[0] // 2
    x, y, z, core = place()

    first, others, own = split_rows(gradient)
    first, others = swap(first, CORE, CORE), swap(others, CORE, CORE)

    def pair(d):
        return own[d].astype(jnp.float32) + (first if d == 2 else others[min(d, 2)]).astype(jnp.float32)

    over_xy, over_z = (0, Y, X, X + Y), (0, Z_NEAR, Z_FAR, Z_NEAR + Z_FAR)
    sent = {2: narrow(pair(2))}
    own, sent[2] = lax.optimization_barrier((own, sent[2]))
    sent.update({d: narrow(pair(d)) for d in (1, 3)})
    got = [swap(sent[d], over_xy[d], over_z[d]) for d in (2, 3, 1)]
    quarter = lax.optimization_barrier(pair(0) + widen(got[0]))
    quarter = quarter + widen(got[1]) + widen(got[2])
    me = jnp.where(core == 0, z, 2 * x + y)
    got = [swap(narrow(pick(quarter, me ^ d)), over_z[d], over_xy[d]) for d in (1, 2, 3)]
    total = pick(quarter, me) + widen(got[0]) + widen(got[1]) + widen(got[2])

    return jnp.concatenate([total[: tile // 2], total[tile // 2 :]], axis=1)


def join_kernel(mine, far, corner, cross, side, other_side, whole, left):
    cols = mine.shape[1]
    me, core = lax.axis_index("hst"), place()[3]
    bits = lambda at_0, at_1: jnp.where(core == 0, at_0, at_1)
    pieces = [(0, mine), (4, far), (bits(3, 7), corner), (bits(7, 3), cross)]
    pieces += [(bits(2, 1) + 4 * i, side.at[i]) for i in (0, 1)]
    pieces += [(bits(1, 2) + 4 * i, other_side.at[i]) for i in (0, 1)]
    copies = []
    for i, (away, block) in enumerate(pieces):
        at = pl.multiple_of((me ^ away) * cols, 128)
        copies.append(pltpu.make_async_copy(block, whole.at[:, pl.ds(at, cols)], left.at[i]))
        copies[-1].start()
    for copy in copies:
        copy.wait()


def gather_blocks(first, mine):
    row_block, col_block = mine.shape
    far = swap(first, Z_FAR, Z_FAR)
    corner, cross = swap(mine, Z_NEAR + Y, Z_FAR + Z_NEAR + Y), swap(mine, Z_FAR + Z_NEAR + Y, Z_NEAR + Y)
    pair = jnp.stack([mine, far])
    side, other_side = swap(pair, Z_NEAR, Y), swap(pair, Y, Z_NEAR)
    whole = pl.pallas_call(
        join_kernel,
        in_specs=[pl.BlockSpec(memory_space=pl.ANY)] * 6,
        out_specs=pl.BlockSpec(memory_space=pl.ANY),
        out_shape=jax.ShapeDtypeStruct((row_block, 8 * col_block), mine.dtype),
        scratch_shapes=[pltpu.SemaphoreType.DMA((8,))],
        compiler_params=pltpu.CompilerParams(vmem_limit_bytes=8 << 20),
        cost_estimate=pl.CostEstimate(flops=0, bytes_accessed=4 * 8 * mine.size, transcendentals=0),
    )(mine, far, corner, cross, side, other_side)
    return whole, corner


def reduce_general(gradient):
    local_count = lax.axis_size("local")
    host_count = lax.axis_size("hst")
    rows, cols = gradient.shape
    row_block, col_block = rows // local_count, cols // host_count
    pieces = lax.all_to_all(
        gradient.reshape(local_count, row_block, cols),
        "local",
        split_axis=0,
        concat_axis=0,
        tiled=True,
    )
    partial_sum = jnp.sum(pieces.astype(jnp.float32), axis=0)
    arrived = lax.all_to_all(
        partial_sum.reshape(row_block, host_count, col_block),
        "hst",
        split_axis=1,
        concat_axis=1,
        tiled=True,
    )
    return jnp.sum(arrived, axis=1)


def adam(grad_total, master, moment_one, moment_two):
    new_one = beta_one * moment_one + (1.0 - beta_one) * grad_total
    new_two = beta_two * moment_two + (1.0 - beta_two) * grad_total * grad_total
    update = new_one / correct_one / (jnp.sqrt(new_two / correct_two) + epsilon)
    new_master = master - learn_rate * (update + decay_rate * master)
    return new_master, new_one, new_two


def local(grads, master, moment_one, moment_two):
    tuned = lax.axis_size("local") == 4 and lax.axis_size("hst") == 8
    gradient = grads[0, 0]
    grad_total = reduce_blocks(gradient) if tuned else reduce_general(gradient)
    first = adam(grad_total, master, moment_one, moment_two)[0].astype(jnp.bfloat16)
    again, first = lax.optimization_barrier((grad_total, first))
    mine = adam(again, master, moment_one, moment_two)[0].astype(jnp.bfloat16)
    if tuned:
        secondary, corner = gather_blocks(first, mine)
    else:
        secondary = corner = lax.all_gather(mine, "hst", axis=1, tiled=True)
    grad_total, _ = lax.optimization_barrier((again, corner))
    new_master, new_one, new_two = adam(grad_total, master, moment_one, moment_two)
    return (grad_total, new_master, new_one, new_two, secondary)


def solution(mesh):
    return jax.shard_map(
        local,
        mesh=mesh,
        in_specs=(
            P("hst", "local", None, None),
            P("local", "hst"),
            P("local", "hst"),
            P("local", "hst"),
        ),
        out_specs=(
            P("local", "hst"),
            P("local", "hst"),
            P("local", "hst"),
            P("local", "hst"),
            P("local", None),
        ),
        check_vma=False,
    )
```

```python
import jax
import jax.numpy as jnp
from jax import lax
from jax.experimental import pallas as pl
from jax.experimental.pallas import tpu as pltpu
from jax.sharding import PartitionSpec as P

beta_one = 0.9
beta_two = 0.95
learn_rate = 0.02
decay_rate = 0.1
epsilon = 1e-08
correct_one = 1.0 - (0.9**50) ** 2
correct_two = 1.0 - (0.95**50) ** 2

wire_scale = 4096.0


def flip_pairs(flips):
    count = lax.axis_size("hst") * lax.axis_size("local")
    return [(i, i ^ flips[i % 2]) for i in range(count)]


def swap(value, *flips):
    return lax.ppermute(value, ("hst", "local"), flip_pairs(flips))


def narrow(value):
    return (value * wire_scale).astype(jnp.float16)


def widen(value):
    return value.astype(jnp.float32) * (1.0 / wire_scale)


def pick(value, index):
    return lax.dynamic_index_in_dim(value, index, 0, keepdims=False)


CORE, X, Y, Z_NEAR, Z_FAR = 1, 2, 4, 8, 16


def place():
    me_local, me_host = lax.axis_index("local"), lax.axis_index("hst")
    return me_local // 2, me_host % 2, me_host // 2, me_local % 2


def rows_of(core, block, i, store):
    tile, half = block.shape[0] // 2, block.shape[1] // 2
    my_x, my_y, my_z, _ = place()
    z, y = i // 2, i % 2
    block = block.astype(jnp.float32)
    for x in (0, 1):
        left, right = block[x * tile : (x + 1) * tile, :half], block[x * tile : (x + 1) * tile, half:]
        rows = [
            jnp.concatenate([left[at : at + tile // 2], right[at : at + tile // 2]], axis=0).astype(jnp.bfloat16)
            for at in (0, tile // 2)
        ]
        over_z = my_z ^ z
        step = jnp.where(core == 0, (2 * my_x + my_y) ^ (2 * x + y), over_z ^ (over_z // 2))
        member = jnp.where(core == 0, z, 2 * x + y)
        store(step, member, jnp.where(core == 0, rows[0], rows[1]))


def theirs_kernel(whole, first, others, landed, arrived):
    half = first.shape[2]
    core = place()[3]
    parts = [pl.ds(2 * i * half, 2 * half) for i in range(8)]
    copies = [
        pltpu.make_async_copy(whole.at[:, part], landed.at[:, part], arrived.at[i])
        for i, part in enumerate(parts)
    ]
    for copy in copies:
        copy.start()

    def store(step, member, rows):
        @pl.when(step == 3)
        def _():
            first[member] = rows

        @pl.when(step != 3)
        def _():
            others[step, member] = rows

    for i in range(8):
        copies[i].wait()
        rows_of(1 - core, landed[:, parts[i]], i, store)


def own_kernel(landed, own):
    half = own.shape[3]
    core = place()[3]

    def store(step, member, rows):
        own[step, member] = rows

    for i in range(8):
        rows_of(core, landed[:, pl.ds(2 * i * half, 2 * half)], i, store)


def call(kernel, operand, space, outs, scratch=()):
    size = operand.size
    return pl.pallas_call(
        kernel,
        in_specs=[pl.BlockSpec(memory_space=space)],
        out_specs=[pl.BlockSpec(memory_space=pltpu.VMEM)] * len(outs),
        out_shape=[pltpu.VMEM(shape, operand.dtype) for shape in outs],
        scratch_shapes=scratch,
        compiler_params=pltpu.CompilerParams(vmem_limit_bytes=8 << 20),
        cost_estimate=pl.CostEstimate(flops=size, bytes_accessed=4 * size, transcendentals=0),
    )(pltpu.with_memory_space_constraint(operand, space))


def split_rows(gradient):
    rows, cols = gradient.shape
    shape = (4, rows // 2, cols // 16)
    first, others, landed = call(
        theirs_kernel,
        gradient,
        pltpu.HBM,
        [shape, (3, *shape), gradient.shape],
        [pltpu.SemaphoreType.DMA((8,))],
    )
    first, others, landed = lax.optimization_barrier((first, others, landed))
    (own,) = call(own_kernel, landed, pltpu.VMEM, [(4, *shape)])
    return first, others, own


def reduce_blocks(gradient):
    tile = gradient.shape[0] // 2
    x, y, z, core = place()

    first, others, own = split_rows(gradient)
    first, others = swap(first, CORE, CORE), swap(others, CORE, CORE)

    def pair(d):
        return own[d].astype(jnp.float32) + (first if d == 3 else others[d]).astype(jnp.float32)

    over_xy, over_z = (0, Y, X, X + Y), (0, Z_NEAR, Z_FAR, Z_NEAR + Z_FAR)
    sent = {3: narrow(pair(3))}
    own, sent[3] = lax.optimization_barrier((own, sent[3]))
    sent.update({d: narrow(pair(d)) for d in (1, 2)})
    got = [swap(sent[d], over_xy[d], over_z[d ^ (d // 2)]) for d in (3, 1, 2)]
    quarter = lax.optimization_barrier(pair(0) + widen(got[0]))
    quarter = quarter + widen(got[1]) + widen(got[2])
    me = jnp.where(core == 0, z, 2 * x + y)
    got = [swap(narrow(pick(quarter, me ^ d)), over_z[d], over_xy[d]) for d in (1, 2, 3)]
    total = pick(quarter, me) + widen(got[0]) + widen(got[1]) + widen(got[2])

    return jnp.concatenate([total[: tile // 2], total[tile // 2 :]], axis=1)


def join_kernel(mine, far, corner, cross, side, other_side, whole, left):
    cols = mine.shape[1]
    me, core = lax.axis_index("hst"), place()[3]
    bits = lambda at_0, at_1: jnp.where(core == 0, at_0, at_1)
    pieces = [(0, mine), (4, far), (bits(3, 7), corner), (bits(7, 3), cross)]
    pieces += [(bits(2, 1) + 4 * i, side.at[i]) for i in (0, 1)]
    pieces += [(bits(1, 2) + 4 * i, other_side.at[i]) for i in (0, 1)]
    copies = []
    for i, (away, block) in enumerate(pieces):
        at = pl.multiple_of((me ^ away) * cols, 128)
        copies.append(pltpu.make_async_copy(block, whole.at[:, pl.ds(at, cols)], left.at[i]))
        copies[-1].start()
    for copy in copies:
        copy.wait()


def gather_blocks(first, mine):
    row_block, col_block = mine.shape
    far = swap(first, Z_FAR, Z_FAR)
    corner, cross = swap(mine, Z_NEAR + Y, Z_FAR + Z_NEAR + Y), swap(mine, Z_FAR + Z_NEAR + Y, Z_NEAR + Y)
    pair = jnp.stack([mine, far])
    side, other_side = swap(pair, Z_NEAR, Y), swap(pair, Y, Z_NEAR)
    whole = pl.pallas_call(
        join_kernel,
        in_specs=[pl.BlockSpec(memory_space=pl.ANY)] * 6,
        out_specs=pl.BlockSpec(memory_space=pl.ANY),
        out_shape=jax.ShapeDtypeStruct((row_block, 8 * col_block), mine.dtype),
        scratch_shapes=[pltpu.SemaphoreType.DMA((8,))],
        compiler_params=pltpu.CompilerParams(vmem_limit_bytes=8 << 20),
        cost_estimate=pl.CostEstimate(flops=0, bytes_accessed=4 * 8 * mine.size, transcendentals=0),
    )(mine, far, corner, cross, side, other_side)
    return whole, corner


def reduce_general(gradient):
    local_count = lax.axis_size("local")
    host_count = lax.axis_size("hst")
    rows, cols = gradient.shape
    row_block, col_block = rows // local_count, cols // host_count
    pieces = lax.all_to_all(
        gradient.reshape(local_count, row_block, cols),
        "local",
        split_axis=0,
        concat_axis=0,
        tiled=True,
    )
    partial_sum = jnp.sum(pieces.astype(jnp.float32), axis=0)
    arrived = lax.all_to_all(
        partial_sum.reshape(row_block, host_count, col_block),
        "hst",
        split_axis=1,
        concat_axis=1,
        tiled=True,
    )
    return jnp.sum(arrived, axis=1)


def adam(grad_total, master, moment_one, moment_two):
    new_one = beta_one * moment_one + (1.0 - beta_one) * grad_total
    new_two = beta_two * moment_two + (1.0 - beta_two) * grad_total * grad_total
    update = new_one / correct_one / (jnp.sqrt(new_two / correct_two) + epsilon)
    new_master = master - learn_rate * (update + decay_rate * master)
    return new_master, new_one, new_two


def local(grads, master, moment_one, moment_two):
    tuned = lax.axis_size("local") == 4 and lax.axis_size("hst") == 8
    gradient = grads[0, 0]
    grad_total = reduce_blocks(gradient) if tuned else reduce_general(gradient)
    first = adam(grad_total, master, moment_one, moment_two)[0].astype(jnp.bfloat16)
    again, first = lax.optimization_barrier((grad_total, first))
    mine = adam(again, master, moment_one, moment_two)[0].astype(jnp.bfloat16)
    if tuned:
        secondary, corner = gather_blocks(first, mine)
    else:
        secondary = corner = lax.all_gather(mine, "hst", axis=1, tiled=True)
    grad_total, _ = lax.optimization_barrier((again, corner))
    new_master, new_one, new_two = adam(grad_total, master, moment_one, moment_two)
    return (grad_total, new_master, new_one, new_two, secondary)


def solution(mesh):
    return jax.shard_map(
        local,
        mesh=mesh,
        in_specs=(
            P("hst", "local", None, None),
            P("local", "hst"),
            P("local", "hst"),
            P("local", "hst"),
        ),
        out_specs=(
            P("local", "hst"),
            P("local", "hst"),
            P("local", "hst"),
            P("local", "hst"),
            P("local", None),
        ),
        check_vma=False,
    )
```

```python
import jax
import jax.numpy as jnp
from jax import lax
from jax.experimental import pallas as pl
from jax.experimental.pallas import tpu as pltpu
from jax.sharding import PartitionSpec as P

beta_one = 0.9
beta_two = 0.95
learn_rate = 0.02
decay_rate = 0.1
epsilon = 1e-08
correct_one = 1.0 - (0.9**50) ** 2
correct_two = 1.0 - (0.95**50) ** 2

wire_scale = 4096.0


def flip_pairs(flips):
    count = lax.axis_size("hst") * lax.axis_size("local")
    return [(i, i ^ flips[i % 2]) for i in range(count)]


def swap(value, *flips):
    return lax.ppermute(value, ("hst", "local"), flip_pairs(flips))


def narrow(value):
    return (value * wire_scale).astype(jnp.float16)


def widen(value):
    return value.astype(jnp.float32) * (1.0 / wire_scale)


def pick(value, index):
    return lax.dynamic_index_in_dim(value, index, 0, keepdims=False)


CORE, X, Y, Z_NEAR, Z_FAR = 1, 2, 4, 8, 16


def place():
    me_local, me_host = lax.axis_index("local"), lax.axis_index("hst")
    return me_local // 2, me_host % 2, me_host // 2, me_local % 2


def rows_of(core, block, i, store):
    tile, half = block.shape[0] // 2, block.shape[1] // 2
    my_x, my_y, my_z, _ = place()
    z, y = i // 2, i % 2
    block = block.astype(jnp.float32)
    for x in (0, 1):
        left, right = block[x * tile : (x + 1) * tile, :half], block[x * tile : (x + 1) * tile, half:]
        rows = [
            jnp.concatenate([left[at : at + tile // 2], right[at : at + tile // 2]], axis=0).astype(jnp.bfloat16)
            for at in (0, tile // 2)
        ]
        over_z = my_z ^ z
        step = jnp.where(core == 0, (2 * my_x + my_y) ^ (2 * x + y), over_z ^ (over_z // 2))
        member = jnp.where(core == 0, z, 2 * x + y)
        store(step, member, jnp.where(core == 0, rows[0], rows[1]))


def theirs_kernel(whole, first, others, landed, arrived):
    half = first.shape[2]
    core = place()[3]
    parts = [pl.ds(2 * i * half, 2 * half) for i in range(8)]
    copies = [
        pltpu.make_async_copy(whole.at[:, part], landed.at[:, part], arrived.at[i])
        for i, part in enumerate(parts)
    ]
    for copy in copies:
        copy.start()

    def store(step, member, rows):
        @pl.when(step == 3)
        def _():
            first[member] = rows

        @pl.when(step != 3)
        def _():
            others[jnp.minimum(step, 2), member] = rows

    for i in range(8):
        copies[i].wait()
        rows_of(1 - core, landed[:, parts[i]], i, store)


def own_kernel(landed, own):
    half = own.shape[3]
    core = place()[3]

    def store(step, member, rows):
        own[step, member] = rows

    for i in range(8):
        rows_of(core, landed[:, pl.ds(2 * i * half, 2 * half)], i, store)


def call(kernel, operand, space, outs, scratch=()):
    size = operand.size
    return pl.pallas_call(
        kernel,
        in_specs=[pl.BlockSpec(memory_space=space)],
        out_specs=[pl.BlockSpec(memory_space=pltpu.VMEM)] * len(outs),
        out_shape=[pltpu.VMEM(shape, operand.dtype) for shape in outs],
        scratch_shapes=scratch,
        compiler_params=pltpu.CompilerParams(vmem_limit_bytes=8 << 20),
        cost_estimate=pl.CostEstimate(flops=size, bytes_accessed=4 * size, transcendentals=0),
    )(pltpu.with_memory_space_constraint(operand, space))


def split_rows(gradient):
    rows, cols = gradient.shape
    shape = (4, rows // 2, cols // 16)
    first, others, landed = call(
        theirs_kernel,
        gradient,
        pltpu.HBM,
        [shape, (3, *shape), gradient.shape],
        [pltpu.SemaphoreType.DMA((8,))],
    )
    first, others, landed = lax.optimization_barrier((first, others, landed))
    (own,) = call(own_kernel, landed, pltpu.VMEM, [(4, *shape)])
    return first, others, own


def reduce_blocks(gradient):
    tile = gradient.shape[0] // 2
    x, y, z, core = place()

    first, others, own = split_rows(gradient)
    first, others = swap(first, CORE, CORE), swap(others, CORE, CORE)

    def pair(d):
        return own[d].astype(jnp.float32) + (first if d == 3 else others[d]).astype(jnp.float32)

    over_xy, over_z = (0, Y, X, X + Y), (0, Z_NEAR, Z_FAR, Z_NEAR + Z_FAR)
    sent = {3: narrow(pair(3))}
    own, sent[3] = lax.optimization_barrier((own, sent[3]))
    sent.update({d: narrow(pair(d)) for d in (1, 2)})
    got = [swap(sent[d], over_xy[d], over_z[d ^ (d // 2)]) for d in (3, 1, 2)]
    quarter = lax.optimization_barrier(pair(0) + widen(got[0]))
    quarter = quarter + widen(got[1]) + widen(got[2])
    me = jnp.where(core == 0, z, 2 * x + y)
    got = [swap(narrow(pick(quarter, me ^ d)), over_z[d], over_xy[d]) for d in (1, 2, 3)]
    total = pick(quarter, me) + widen(got[0]) + widen(got[1]) + widen(got[2])

    return jnp.concatenate([total[: tile // 2], total[tile // 2 :]], axis=1)


def join_kernel(mine, far, corner, cross, side, other_side, whole, left):
    cols = mine.shape[1]
    me, core = lax.axis_index("hst"), place()[3]
    bits = lambda at_0, at_1: jnp.where(core == 0, at_0, at_1)
    pieces = [(0, mine), (4, far), (bits(3, 7), corner), (bits(7, 3), cross)]
    pieces += [(bits(2, 1) + 4 * i, side.at[i]) for i in (0, 1)]
    pieces += [(bits(1, 2) + 4 * i, other_side.at[i]) for i in (0, 1)]
    copies = []
    for i, (away, block) in enumerate(pieces):
        at = pl.multiple_of((me ^ away) * cols, 128)
        copies.append(pltpu.make_async_copy(block, whole.at[:, pl.ds(at, cols)], left.at[i]))
        copies[-1].start()
    for copy in copies:
        copy.wait()


def gather_blocks(mine):
    row_block, col_block = mine.shape
    far = swap(mine, Z_FAR, Z_FAR)
    corner, cross = swap(mine, Z_NEAR + Y, Z_FAR + Z_NEAR + Y), swap(mine, Z_FAR + Z_NEAR + Y, Z_NEAR + Y)
    pair = jnp.stack([mine, far])
    side, other_side = swap(pair, Z_NEAR, Y), swap(pair, Y, Z_NEAR)
    whole = pl.pallas_call(
        join_kernel,
        in_specs=[pl.BlockSpec(memory_space=pl.ANY)] * 6,
        out_specs=pl.BlockSpec(memory_space=pl.ANY),
        out_shape=jax.ShapeDtypeStruct((row_block, 8 * col_block), mine.dtype),
        scratch_shapes=[pltpu.SemaphoreType.DMA((8,))],
        compiler_params=pltpu.CompilerParams(vmem_limit_bytes=8 << 20),
        cost_estimate=pl.CostEstimate(flops=0, bytes_accessed=4 * 8 * mine.size, transcendentals=0),
    )(mine, far, corner, cross, side, other_side)
    return whole, corner


def reduce_general(gradient):
    local_count = lax.axis_size("local")
    host_count = lax.axis_size("hst")
    rows, cols = gradient.shape
    row_block, col_block = rows // local_count, cols // host_count
    pieces = lax.all_to_all(
        gradient.reshape(local_count, row_block, cols),
        "local",
        split_axis=0,
        concat_axis=0,
        tiled=True,
    )
    partial_sum = jnp.sum(pieces.astype(jnp.float32), axis=0)
    arrived = lax.all_to_all(
        partial_sum.reshape(row_block, host_count, col_block),
        "hst",
        split_axis=1,
        concat_axis=1,
        tiled=True,
    )
    return jnp.sum(arrived, axis=1)


def adam(grad_total, master, moment_one, moment_two):
    new_one = beta_one * moment_one + (1.0 - beta_one) * grad_total
    new_two = beta_two * moment_two + (1.0 - beta_two) * grad_total * grad_total
    update = new_one / correct_one / (jnp.sqrt(new_two / correct_two) + epsilon)
    new_master = master - learn_rate * (update + decay_rate * master)
    return new_master, new_one, new_two


def local(grads, master, moment_one, moment_two):
    tuned = lax.axis_size("local") == 4 and lax.axis_size("hst") == 8
    gradient = grads[0, 0]
    grad_total = reduce_blocks(gradient) if tuned else reduce_general(gradient)
    mine = adam(grad_total, master, moment_one, moment_two)[0].astype(jnp.bfloat16)
    if tuned:
        secondary, corner = gather_blocks(mine)
    else:
        secondary = corner = lax.all_gather(mine, "hst", axis=1, tiled=True)
    grad_total, _ = lax.optimization_barrier((grad_total, corner))
    new_master, new_one, new_two = adam(grad_total, master, moment_one, moment_two)
    return (grad_total, new_master, new_one, new_two, secondary)


def solution(mesh):
    return jax.shard_map(
        local,
        mesh=mesh,
        in_specs=(
            P("hst", "local", None, None),
            P("local", "hst"),
            P("local", "hst"),
            P("local", "hst"),
        ),
        out_specs=(
            P("local", "hst"),
            P("local", "hst"),
            P("local", "hst"),
            P("local", "hst"),
            P("local", None),
        ),
        check_vma=False,
    )
```

```python
import jax
import jax.numpy as jnp
from jax import lax
from jax.experimental import pallas as pl
from jax.experimental.pallas import tpu as pltpu
from jax.sharding import PartitionSpec as P

beta_one = 0.9
beta_two = 0.95
learn_rate = 0.02
decay_rate = 0.1
epsilon = 1e-08
correct_one = 1.0 - (0.9**50) ** 2
correct_two = 1.0 - (0.95**50) ** 2

wire_scale = 4096.0


def flip_pairs(flips):
    count = lax.axis_size("hst") * lax.axis_size("local")
    return [(i, i ^ flips[i % 2]) for i in range(count)]


def swap(value, *flips):
    return lax.ppermute(value, ("hst", "local"), flip_pairs(flips))


def narrow(value):
    return (value * wire_scale).astype(jnp.float16)


def widen(value):
    return value.astype(jnp.float32) * (1.0 / wire_scale)


def pick(value, index):
    return lax.dynamic_index_in_dim(value, index, 0, keepdims=False)


CORE, X, Y, Z_NEAR, Z_FAR = 1, 2, 4, 8, 16


def place():
    me_local, me_host = lax.axis_index("local"), lax.axis_index("hst")
    return me_local // 2, me_host % 2, me_host // 2, me_local % 2


def rows_of(core, block, i, store):
    tile, half = block.shape[0] // 2, block.shape[1] // 2
    my_x, my_y, my_z, _ = place()
    z, y = i // 2, i % 2
    block = block.astype(jnp.float32)
    for x in (0, 1):
        left, right = block[x * tile : (x + 1) * tile, :half], block[x * tile : (x + 1) * tile, half:]
        rows = [
            jnp.concatenate([left[at : at + tile // 2], right[at : at + tile // 2]], axis=0).astype(jnp.bfloat16)
            for at in (0, tile // 2)
        ]
        over_z = my_z ^ z
        step = jnp.where(core == 0, (2 * my_x + my_y) ^ (2 * x + y), over_z ^ (over_z // 2))
        member = jnp.where(core == 0, z, 2 * x + y)
        store(step, member, jnp.where(core == 0, rows[0], rows[1]))


def theirs_kernel(whole, first, others, landed, arrived):
    half = first.shape[2]
    core = place()[3]
    parts = [pl.ds(2 * i * half, 2 * half) for i in range(8)]
    copies = [
        pltpu.make_async_copy(whole.at[:, part], landed.at[:, part], arrived.at[i])
        for i, part in enumerate(parts)
    ]
    for copy in copies:
        copy.start()

    def store(step, member, rows):
        @pl.when(step == 3)
        def _():
            first[member] = rows

        @pl.when(step != 3)
        def _():
            others[jnp.minimum(step, 2), member] = rows

    for i in range(8):
        copies[i].wait()
        rows_of(1 - core, landed[:, parts[i]], i, store)


def own_kernel(landed, own):
    half = own.shape[3]
    core = place()[3]

    def store(step, member, rows):
        own[step, member] = rows

    for i in range(8):
        rows_of(core, landed[:, pl.ds(2 * i * half, 2 * half)], i, store)


def call(kernel, operand, space, outs, scratch=()):
    size = operand.size
    return pl.pallas_call(
        kernel,
        in_specs=[pl.BlockSpec(memory_space=space)],
        out_specs=[pl.BlockSpec(memory_space=pltpu.VMEM)] * len(outs),
        out_shape=[pltpu.VMEM(shape, operand.dtype) for shape in outs],
        scratch_shapes=scratch,
        compiler_params=pltpu.CompilerParams(vmem_limit_bytes=8 << 20),
        cost_estimate=pl.CostEstimate(flops=size, bytes_accessed=4 * size, transcendentals=0),
    )(pltpu.with_memory_space_constraint(operand, space))


def split_rows(gradient):
    rows, cols = gradient.shape
    shape = (4, rows // 2, cols // 16)
    first, others, landed = call(
        theirs_kernel,
        gradient,
        pltpu.HBM,
        [shape, (3, *shape), gradient.shape],
        [pltpu.SemaphoreType.DMA((8,))],
    )
    first, others, landed = lax.optimization_barrier((first, others, landed))
    (own,) = call(own_kernel, landed, pltpu.VMEM, [(4, *shape)])
    return first, others, own


def reduce_blocks(gradient):
    tile = gradient.shape[0] // 2
    x, y, z, core = place()

    first, others, own = split_rows(gradient)
    first, others = swap(first, CORE, CORE), swap(others, CORE, CORE)

    def pair(d):
        return own[d].astype(jnp.float32) + (first if d == 3 else others[d]).astype(jnp.float32)

    over_xy, over_z = (0, Y, X, X + Y), (0, Z_NEAR, Z_FAR, Z_NEAR + Z_FAR)
    sent = {3: narrow(pair(3))}
    own, sent[3] = lax.optimization_barrier((own, sent[3]))
    sent.update({d: narrow(pair(d)) for d in (1, 2)})
    got = [swap(sent[d], over_xy[d], over_z[d ^ (d // 2)]) for d in (3, 1, 2)]
    quarter = lax.optimization_barrier(pair(0) + widen(got[0]))
    quarter = quarter + widen(got[1]) + widen(got[2])
    me = jnp.where(core == 0, z, 2 * x + y)
    got = [swap(narrow(pick(quarter, me ^ d)), over_z[d], over_xy[d]) for d in (1, 2, 3)]
    total = pick(quarter, me) + widen(got[0]) + widen(got[1]) + widen(got[2])

    return jnp.concatenate([total[: tile // 2], total[tile // 2 :]], axis=1)


def join_kernel(mine, far, corner, cross, side, other_side, whole, left):
    cols = mine.shape[1]
    me, core = lax.axis_index("hst"), place()[3]
    bits = lambda at_0, at_1: jnp.where(core == 0, at_0, at_1)
    pieces = [(0, mine), (4, far), (3, corner), (7, cross)]
    pieces += [(bits(2, 1) + 4 * i, side.at[i]) for i in (0, 1)]
    pieces += [(bits(1, 2) + 4 * i, other_side.at[i]) for i in (0, 1)]
    copies = []
    for i, (away, block) in enumerate(pieces):
        at = pl.multiple_of((me ^ away) * cols, 128)
        copies.append(pltpu.make_async_copy(block, whole.at[:, pl.ds(at, cols)], left.at[i]))
        copies[-1].start()
    for copy in copies:
        copy.wait()


def gather_blocks(mine):
    row_block, col_block = mine.shape
    far = swap(mine, Z_FAR, Z_FAR)
    corner, cross = [swap(mine, to, to) for to in (Z_NEAR + Y, Z_FAR + Z_NEAR + Y)]
    pair = jnp.stack([mine, far])
    side, other_side = swap(pair, Z_NEAR, Y), swap(pair, Y, Z_NEAR)
    whole = pl.pallas_call(
        join_kernel,
        in_specs=[pl.BlockSpec(memory_space=pl.ANY)] * 6,
        out_specs=pl.BlockSpec(memory_space=pl.ANY),
        out_shape=jax.ShapeDtypeStruct((row_block, 8 * col_block), mine.dtype),
        scratch_shapes=[pltpu.SemaphoreType.DMA((8,))],
        compiler_params=pltpu.CompilerParams(vmem_limit_bytes=8 << 20),
        cost_estimate=pl.CostEstimate(flops=0, bytes_accessed=4 * 8 * mine.size, transcendentals=0),
    )(mine, far, corner, cross, side, other_side)
    return whole, corner


def reduce_general(gradient):
    local_count = lax.axis_size("local")
    host_count = lax.axis_size("hst")
    rows, cols = gradient.shape
    row_block, col_block = rows // local_count, cols // host_count
    pieces = lax.all_to_all(
        gradient.reshape(local_count, row_block, cols),
        "local",
        split_axis=0,
        concat_axis=0,
        tiled=True,
    )
    partial_sum = jnp.sum(pieces.astype(jnp.float32), axis=0)
    arrived = lax.all_to_all(
        partial_sum.reshape(row_block, host_count, col_block),
        "hst",
        split_axis=1,
        concat_axis=1,
        tiled=True,
    )
    return jnp.sum(arrived, axis=1)


def adam(grad_total, master, moment_one, moment_two):
    new_one = beta_one * moment_one + (1.0 - beta_one) * grad_total
    new_two = beta_two * moment_two + (1.0 - beta_two) * grad_total * grad_total
    update = new_one / correct_one / (jnp.sqrt(new_two / correct_two) + epsilon)
    new_master = master - learn_rate * (update + decay_rate * master)
    return new_master, new_one, new_two


def local(grads, master, moment_one, moment_two):
    tuned = lax.axis_size("local") == 4 and lax.axis_size("hst") == 8
    gradient = grads[0, 0]
    grad_total = reduce_blocks(gradient) if tuned else reduce_general(gradient)
    mine = adam(grad_total, master, moment_one, moment_two)[0].astype(jnp.bfloat16)
    if tuned:
        secondary, corner = gather_blocks(mine)
    else:
        secondary = corner = lax.all_gather(mine, "hst", axis=1, tiled=True)
    grad_total, _ = lax.optimization_barrier((grad_total, corner))
    new_master, new_one, new_two = adam(grad_total, master, moment_one, moment_two)
    return (grad_total, new_master, new_one, new_two, secondary)


def solution(mesh):
    return jax.shard_map(
        local,
        mesh=mesh,
        in_specs=(
            P("hst", "local", None, None),
            P("local", "hst"),
            P("local", "hst"),
            P("local", "hst"),
        ),
        out_specs=(
            P("local", "hst"),
            P("local", "hst"),
            P("local", "hst"),
            P("local", "hst"),
            P("local", None),
        ),
        check_vma=False,
    )
```

```python
import jax
import jax.numpy as jnp
from jax import lax
from jax.experimental import pallas as pl
from jax.experimental.pallas import tpu as pltpu
from jax.sharding import PartitionSpec as P

beta_one = 0.9
beta_two = 0.95
learn_rate = 0.02
decay_rate = 0.1
epsilon = 1e-08
correct_one = 1.0 - (0.9**50) ** 2
correct_two = 1.0 - (0.95**50) ** 2

wire_scale = 4096.0


def flip_pairs(flips):
    count = lax.axis_size("hst") * lax.axis_size("local")
    return [(i, i ^ flips[i % 2]) for i in range(count)]


def swap(value, *flips):
    return lax.ppermute(value, ("hst", "local"), flip_pairs(flips))


def narrow(value):
    return (value * wire_scale).astype(jnp.float16)


def widen(value):
    return value.astype(jnp.float32) * (1.0 / wire_scale)


def pick(value, index):
    return lax.dynamic_index_in_dim(value, index, 0, keepdims=False)


CORE, X, Y, Z_NEAR, Z_FAR = 1, 2, 4, 8, 16


def place():
    me_local, me_host = lax.axis_index("local"), lax.axis_index("hst")
    return me_local // 2, me_host % 2, me_host // 2, me_local % 2


def rows_of(core, block, i, store):
    tile, half = block.shape[0] // 2, block.shape[1] // 2
    my_x, my_y, my_z, _ = place()
    z, y = i // 2, i % 2
    block = block.astype(jnp.float32)
    for x in (0, 1):
        left, right = block[x * tile : (x + 1) * tile, :half], block[x * tile : (x + 1) * tile, half:]
        rows = [
            jnp.concatenate([left[at : at + tile // 2], right[at : at + tile // 2]], axis=0).astype(jnp.bfloat16)
            for at in (0, tile // 2)
        ]
        over_z = my_z ^ z
        step = jnp.where(core == 0, (2 * my_x + my_y) ^ (2 * x + y), over_z ^ (over_z // 2))
        member = jnp.where(core == 0, z, 2 * x + y)
        store(step, member, jnp.where(core == 0, rows[0], rows[1]))


def theirs_kernel(whole, first, others, landed, arrived):
    half = first.shape[2]
    core = place()[3]
    parts = [pl.ds(2 * i * half, 2 * half) for i in range(8)]
    copies = [
        pltpu.make_async_copy(whole.at[:, part], landed.at[:, part], arrived.at[i])
        for i, part in enumerate(parts)
    ]
    for copy in copies:
        copy.start()

    def store(step, member, rows):
        @pl.when(step == 3)
        def _():
            first[member] = rows

        @pl.when(step != 3)
        def _():
            others[jnp.minimum(step, 2), member] = rows

    for i in range(8):
        copies[i].wait()
        rows_of(1 - core, landed[:, parts[i]], i, store)


def own_kernel(landed, own):
    half = own.shape[3]
    core = place()[3]

    def store(step, member, rows):
        own[step, member] = rows

    for i in range(8):
        rows_of(core, landed[:, pl.ds(2 * i * half, 2 * half)], i, store)


def call(kernel, operand, space, outs, scratch=()):
    size = operand.size
    return pl.pallas_call(
        kernel,
        in_specs=[pl.BlockSpec(memory_space=space)],
        out_specs=[pl.BlockSpec(memory_space=pltpu.VMEM)] * len(outs),
        out_shape=[pltpu.VMEM(shape, operand.dtype) for shape in outs],
        scratch_shapes=scratch,
        compiler_params=pltpu.CompilerParams(vmem_limit_bytes=8 << 20),
        cost_estimate=pl.CostEstimate(flops=size, bytes_accessed=4 * size, transcendentals=0),
    )(pltpu.with_memory_space_constraint(operand, space))


def split_rows(gradient):
    rows, cols = gradient.shape
    shape = (4, rows // 2, cols // 16)
    first, others, landed = call(
        theirs_kernel,
        gradient,
        pltpu.HBM,
        [shape, (3, *shape), gradient.shape],
        [pltpu.SemaphoreType.DMA((8,))],
    )
    first, others, landed = lax.optimization_barrier((first, others, landed))
    (own,) = call(own_kernel, landed, pltpu.VMEM, [(4, *shape)])
    return first, others, own


def reduce_blocks(gradient):
    tile = gradient.shape[0] // 2
    x, y, z, core = place()

    first, others, own = split_rows(gradient)
    first, others = swap(first, CORE, CORE), swap(others, CORE, CORE)

    def pair(d):
        return own[d].astype(jnp.float32) + (first if d == 3 else others[d]).astype(jnp.float32)

    over_xy, over_z = (0, Y, X, X + Y), (0, Z_NEAR, Z_FAR, Z_NEAR + Z_FAR)
    sent = {3: narrow(pair(3))}
    own, sent[3] = lax.optimization_barrier((own, sent[3]))
    sent.update({d: narrow(pair(d)) for d in (1, 2)})
    got = [swap(sent[d], over_xy[d], over_z[d ^ (d // 2)]) for d in (3, 1, 2)]
    quarter = lax.optimization_barrier(pair(0) + widen(got[0]))
    quarter = quarter + widen(got[1]) + widen(got[2])
    me = jnp.where(core == 0, z, 2 * x + y)
    got = [swap(narrow(pick(quarter, me ^ d)), over_z[d], over_xy[d]) for d in (1, 2, 3)]
    total = pick(quarter, me) + widen(got[0]) + widen(got[1]) + widen(got[2])

    return jnp.concatenate([total[: tile // 2], total[tile // 2 :]], axis=1)


def join_kernel(mine, far, beside, cross, three, small, whole, left):
    cols = mine.shape[1]
    me, core = lax.axis_index("hst"), place()[3]
    bits = lambda at_0, at_1: jnp.where(core == 0, at_0, at_1)
    pieces = [(0, mine), (4, far), (bits(2, 1), beside), (7, cross)]
    pieces += [(bits(1, 2), three.at[0]), (bits(5, 6), three.at[1]), (3, three.at[2]), (bits(6, 5), small)]
    copies = []
    for i, (away, block) in enumerate(pieces):
        at = pl.multiple_of((me ^ away) * cols, 128)
        copies.append(pltpu.make_async_copy(block, whole.at[:, pl.ds(at, cols)], left.at[i]))
        copies[-1].start()
    for copy in copies:
        copy.wait()


def gather_blocks(mine):
    row_block, col_block = mine.shape
    far = swap(mine, Z_FAR, Z_FAR)
    beside = swap(mine, Z_NEAR, Y)
    cross = swap(mine, Z_FAR + Z_NEAR + Y, Z_FAR + Z_NEAR + Y)
    three = swap(jnp.stack([mine, far, beside]), Y, Z_NEAR)
    small = swap(far, Z_NEAR, Y)
    whole = pl.pallas_call(
        join_kernel,
        in_specs=[pl.BlockSpec(memory_space=pl.ANY)] * 6,
        out_specs=pl.BlockSpec(memory_space=pl.ANY),
        out_shape=jax.ShapeDtypeStruct((row_block, 8 * col_block), mine.dtype),
        scratch_shapes=[pltpu.SemaphoreType.DMA((8,))],
        compiler_params=pltpu.CompilerParams(vmem_limit_bytes=8 << 20),
        cost_estimate=pl.CostEstimate(flops=0, bytes_accessed=4 * 8 * mine.size, transcendentals=0),
    )(mine, far, beside, cross, three, small)
    return whole, far


def reduce_general(gradient):
    local_count = lax.axis_size("local")
    host_count = lax.axis_size("hst")
    rows, cols = gradient.shape
    row_block, col_block = rows // local_count, cols // host_count
    pieces = lax.all_to_all(
        gradient.reshape(local_count, row_block, cols),
        "local",
        split_axis=0,
        concat_axis=0,
        tiled=True,
    )
    partial_sum = jnp.sum(pieces.astype(jnp.float32), axis=0)
    arrived = lax.all_to_all(
        partial_sum.reshape(row_block, host_count, col_block),
        "hst",
        split_axis=1,
        concat_axis=1,
        tiled=True,
    )
    return jnp.sum(arrived, axis=1)


def adam(grad_total, master, moment_one, moment_two):
    new_one = beta_one * moment_one + (1.0 - beta_one) * grad_total
    new_two = beta_two * moment_two + (1.0 - beta_two) * grad_total * grad_total
    update = new_one / correct_one / (jnp.sqrt(new_two / correct_two) + epsilon)
    new_master = master - learn_rate * (update + decay_rate * master)
    return new_master, new_one, new_two


def local(grads, master, moment_one, moment_two):
    tuned = lax.axis_size("local") == 4 and lax.axis_size("hst") == 8
    gradient = grads[0, 0]
    grad_total = reduce_blocks(gradient) if tuned else reduce_general(gradient)
    mine = adam(grad_total, master, moment_one, moment_two)[0].astype(jnp.bfloat16)
    if tuned:
        secondary, early = gather_blocks(mine)
    else:
        secondary = early = lax.all_gather(mine, "hst", axis=1, tiled=True)
    grad_total, _ = lax.optimization_barrier((grad_total, early))
    new_master, new_one, new_two = adam(grad_total, master, moment_one, moment_two)
    return (grad_total, new_master, new_one, new_two, secondary)


def solution(mesh):
    return jax.shard_map(
        local,
        mesh=mesh,
        in_specs=(
            P("hst", "local", None, None),
            P("local", "hst"),
            P("local", "hst"),
            P("local", "hst"),
        ),
        out_specs=(
            P("local", "hst"),
            P("local", "hst"),
            P("local", "hst"),
            P("local", "hst"),
            P("local", None),
        ),
        check_vma=False,
    )
```

```python
import jax
import jax.numpy as jnp
from jax import lax
from jax.experimental import pallas as pl
from jax.experimental.pallas import tpu as pltpu
from jax.sharding import PartitionSpec as P

beta_one = 0.9
beta_two = 0.95
learn_rate = 0.02
decay_rate = 0.1
epsilon = 1e-08
correct_one = 1.0 - (0.9**50) ** 2
correct_two = 1.0 - (0.95**50) ** 2

wire_scale = 4096.0


def flip_pairs(flips):
    count = lax.axis_size("hst") * lax.axis_size("local")
    return [(i, i ^ flips[i % 2]) for i in range(count)]


def swap(value, *flips):
    return lax.ppermute(value, ("hst", "local"), flip_pairs(flips))


def narrow(value):
    return (value * wire_scale).astype(jnp.float16)


def widen(value):
    return value.astype(jnp.float32) * (1.0 / wire_scale)


def pick(value, index):
    return lax.dynamic_index_in_dim(value, index, 0, keepdims=False)


CORE, X, Y, Z_NEAR, Z_FAR = 1, 2, 4, 8, 16


def place():
    me_local, me_host = lax.axis_index("local"), lax.axis_index("hst")
    return me_local // 2, me_host % 2, me_host // 2, me_local % 2


def rows_of(core, block, i, store):
    tile, half = block.shape[0] // 2, block.shape[1] // 2
    my_x, my_y, my_z, _ = place()
    z, y = i // 2, i % 2
    block = block.astype(jnp.float32)
    for x in (0, 1):
        left, right = block[x * tile : (x + 1) * tile, :half], block[x * tile : (x + 1) * tile, half:]
        rows = [
            jnp.concatenate([left[at : at + tile // 2], right[at : at + tile // 2]], axis=0).astype(jnp.bfloat16)
            for at in (0, tile // 2)
        ]
        over_z = my_z ^ z
        step = jnp.where(core == 0, (2 * my_x + my_y) ^ (2 * x + y), over_z ^ (over_z // 2))
        member = jnp.where(core == 0, z, 2 * x + y)
        store(step, member, jnp.where(core == 0, rows[0], rows[1]))


def theirs_kernel(whole, first, others, landed, arrived):
    half = first.shape[2]
    core = place()[3]
    parts = [pl.ds(2 * i * half, 2 * half) for i in range(8)]
    copies = [
        pltpu.make_async_copy(whole.at[:, part], landed.at[:, part], arrived.at[i])
        for i, part in enumerate(parts)
    ]
    for copy in copies:
        copy.start()

    def store(step, member, rows):
        @pl.when(step == 3)
        def _():
            first[member] = rows

        @pl.when(step != 3)
        def _():
            others[jnp.minimum(step, 2), member] = rows

    for i in range(8):
        copies[i].wait()
        rows_of(1 - core, landed[:, parts[i]], i, store)


def own_kernel(landed, own):
    half = own.shape[3]
    core = place()[3]

    def store(step, member, rows):
        own[step, member] = rows

    for i in range(8):
        rows_of(core, landed[:, pl.ds(2 * i * half, 2 * half)], i, store)


def call(kernel, operand, space, outs, scratch=()):
    size = operand.size
    return pl.pallas_call(
        kernel,
        in_specs=[pl.BlockSpec(memory_space=space)],
        out_specs=[pl.BlockSpec(memory_space=pltpu.VMEM)] * len(outs),
        out_shape=[pltpu.VMEM(shape, operand.dtype) for shape in outs],
        scratch_shapes=scratch,
        compiler_params=pltpu.CompilerParams(vmem_limit_bytes=8 << 20),
        cost_estimate=pl.CostEstimate(flops=size, bytes_accessed=4 * size, transcendentals=0),
    )(pltpu.with_memory_space_constraint(operand, space))


def split_rows(gradient):
    rows, cols = gradient.shape
    shape = (4, rows // 2, cols // 16)
    first, others, landed = call(
        theirs_kernel,
        gradient,
        pltpu.HBM,
        [shape, (3, *shape), gradient.shape],
        [pltpu.SemaphoreType.DMA((8,))],
    )
    first, others, landed = lax.optimization_barrier((first, others, landed))
    (own,) = call(own_kernel, landed, pltpu.VMEM, [(4, *shape)])
    return first, others, own


def reduce_blocks(gradient):
    tile = gradient.shape[0] // 2
    x, y, z, core = place()

    first, others, own = split_rows(gradient)
    first, others = swap(first, CORE, CORE), swap(others, CORE, CORE)

    def pair(d):
        return own[d].astype(jnp.float32) + (first if d == 3 else others[d]).astype(jnp.float32)

    over_xy, over_z = (0, Y, X, X + Y), (0, Z_NEAR, Z_FAR, Z_NEAR + Z_FAR)
    sent = {3: narrow(pair(3))}
    own, sent[3] = lax.optimization_barrier((own, sent[3]))
    sent.update({d: narrow(pair(d)) for d in (1, 2)})
    got = [swap(sent[d], over_xy[d], over_z[d ^ (d // 2)]) for d in (3, 1, 2)]
    quarter = lax.optimization_barrier(pair(0) + widen(got[0]))
    quarter = quarter + widen(got[1]) + widen(got[2])
    me = jnp.where(core == 0, z, 2 * x + y)
    got = [swap(narrow(pick(quarter, me ^ d)), over_z[d], over_xy[d]) for d in (1, 3, 2)]
    total = pick(quarter, me) + widen(got[0]) + widen(got[1]) + widen(got[2])

    return jnp.concatenate([total[: tile // 2], total[tile // 2 :]], axis=1)


def join_kernel(mine, far, corner, cross, side, other_side, whole, left):
    cols = mine.shape[1]
    me, core = lax.axis_index("hst"), place()[3]
    bits = lambda at_0, at_1: jnp.where(core == 0, at_0, at_1)
    pieces = [(0, mine), (4, far), (bits(3, 7), corner), (bits(7, 3), cross)]
    pieces += [(bits(2, 1) + 4 * i, side.at[i]) for i in (0, 1)]
    pieces += [(bits(1, 2) + 4 * i, other_side.at[i]) for i in (0, 1)]
    copies = []
    for i, (away, block) in enumerate(pieces):
        at = pl.multiple_of((me ^ away) * cols, 128)
        copies.append(pltpu.make_async_copy(block, whole.at[:, pl.ds(at, cols)], left.at[i]))
        copies[-1].start()
    for copy in copies:
        copy.wait()


def gather_blocks(mine):
    row_block, col_block = mine.shape
    far = swap(mine, Z_FAR, Z_FAR)
    corner, cross = swap(mine, Z_NEAR + Y, Z_FAR + Z_NEAR + Y), swap(mine, Z_FAR + Z_NEAR + Y, Z_NEAR + Y)
    pair = jnp.stack([mine, far])
    side, other_side = swap(pair, Z_NEAR, Y), swap(pair, Y, Z_NEAR)
    whole = pl.pallas_call(
        join_kernel,
        in_specs=[pl.BlockSpec(memory_space=pl.ANY)] * 6,
        out_specs=pl.BlockSpec(memory_space=pl.ANY),
        out_shape=jax.ShapeDtypeStruct((row_block, 8 * col_block), mine.dtype),
        scratch_shapes=[pltpu.SemaphoreType.DMA((8,))],
        compiler_params=pltpu.CompilerParams(vmem_limit_bytes=8 << 20),
        cost_estimate=pl.CostEstimate(flops=0, bytes_accessed=4 * 8 * mine.size, transcendentals=0),
    )(mine, far, corner, cross, side, other_side)
    return whole, corner


def reduce_general(gradient):
    local_count = lax.axis_size("local")
    host_count = lax.axis_size("hst")
    rows, cols = gradient.shape
    row_block, col_block = rows // local_count, cols // host_count
    pieces = lax.all_to_all(
        gradient.reshape(local_count, row_block, cols),
        "local",
        split_axis=0,
        concat_axis=0,
        tiled=True,
    )
    partial_sum = jnp.sum(pieces.astype(jnp.float32), axis=0)
    arrived = lax.all_to_all(
        partial_sum.reshape(row_block, host_count, col_block),
        "hst",
        split_axis=1,
        concat_axis=1,
        tiled=True,
    )
    return jnp.sum(arrived, axis=1)


def adam(grad_total, master, moment_one, moment_two):
    new_one = beta_one * moment_one + (1.0 - beta_one) * grad_total
    new_two = beta_two * moment_two + (1.0 - beta_two) * grad_total * grad_total
    update = new_one / correct_one / (jnp.sqrt(new_two / correct_two) + epsilon)
    new_master = master - learn_rate * (update + decay_rate * master)
    return new_master, new_one, new_two


def local(grads, master, moment_one, moment_two):
    tuned = lax.axis_size("local") == 4 and lax.axis_size("hst") == 8
    gradient = grads[0, 0]
    grad_total = reduce_blocks(gradient) if tuned else reduce_general(gradient)
    mine = adam(grad_total, master, moment_one, moment_two)[0].astype(jnp.bfloat16)
    if tuned:
        secondary, corner = gather_blocks(mine)
    else:
        secondary = corner = lax.all_gather(mine, "hst", axis=1, tiled=True)
    grad_total, _ = lax.optimization_barrier((grad_total, corner))
    new_master, new_one, new_two = adam(grad_total, master, moment_one, moment_two)
    return (grad_total, new_master, new_one, new_two, secondary)


def solution(mesh):
    return jax.shard_map(
        local,
        mesh=mesh,
        in_specs=(
            P("hst", "local", None, None),
            P("local", "hst"),
            P("local", "hst"),
            P("local", "hst"),
        ),
        out_specs=(
            P("local", "hst"),
            P("local", "hst"),
            P("local", "hst"),
            P("local", "hst"),
            P("local", None),
        ),
        check_vma=False,
    )
```

```python
import jax
import jax.numpy as jnp
from jax import lax
from jax.experimental import pallas as pl
from jax.experimental.pallas import tpu as pltpu
from jax.sharding import PartitionSpec as P

beta_one = 0.9
beta_two = 0.95
learn_rate = 0.02
decay_rate = 0.1
epsilon = 1e-08
correct_one = 1.0 - (0.9**50) ** 2
correct_two = 1.0 - (0.95**50) ** 2

wire_scale = 4096.0


def flip_pairs(flips):
    count = lax.axis_size("hst") * lax.axis_size("local")
    return [(i, i ^ flips[i % 2]) for i in range(count)]


def swap(value, *flips):
    return lax.ppermute(value, ("hst", "local"), flip_pairs(flips))


def narrow(value):
    return (value * wire_scale).astype(jnp.float16)


def widen(value):
    return value.astype(jnp.float32) * (1.0 / wire_scale)


def pick(value, index):
    return lax.dynamic_index_in_dim(value, index, 0, keepdims=False)


CORE, X, Y, Z_NEAR, Z_FAR = 1, 2, 4, 8, 16


def place():
    me_local, me_host = lax.axis_index("local"), lax.axis_index("hst")
    return me_local // 2, me_host % 2, me_host // 2, me_local % 2


def rows_of(core, block, i, store):
    tile, half = block.shape[0] // 2, block.shape[1] // 2
    my_x, my_y, my_z, _ = place()
    z, y = i // 2, i % 2
    block = block.astype(jnp.float32)
    for x in (0, 1):
        left, right = block[x * tile : (x + 1) * tile, :half], block[x * tile : (x + 1) * tile, half:]
        rows = [
            jnp.concatenate([left[at : at + tile // 2], right[at : at + tile // 2]], axis=0).astype(jnp.bfloat16)
            for at in (0, tile // 2)
        ]
        over_z = my_z ^ z
        step = jnp.where(core == 0, (2 * my_x + my_y) ^ (2 * x + y), over_z ^ (over_z // 2))
        member = jnp.where(core == 0, z, 2 * x + y)
        store(step, member, jnp.where(core == 0, rows[0], rows[1]))


def theirs_kernel(whole, first, every, landed, arrived):
    half = first.shape[2]
    core = place()[3]
    parts = [pl.ds(2 * i * half, 2 * half) for i in range(8)]
    copies = [
        pltpu.make_async_copy(whole.at[:, part], landed.at[:, part], arrived.at[i])
        for i, part in enumerate(parts)
    ]
    for copy in copies:
        copy.start()

    def store(step, member, rows):
        every[step, member] = rows

    for i in range(8):
        copies[i].wait()
        rows_of(1 - core, landed[:, parts[i]], i, store)
    first[...] = every[3]


def own_kernel(landed, own):
    half = own.shape[3]
    core = place()[3]

    def store(step, member, rows):
        own[step, member] = rows

    for i in range(8):
        rows_of(core, landed[:, pl.ds(2 * i * half, 2 * half)], i, store)


def call(kernel, operand, space, outs, scratch=()):
    size = operand.size
    return pl.pallas_call(
        kernel,
        in_specs=[pl.BlockSpec(memory_space=space)],
        out_specs=[pl.BlockSpec(memory_space=pltpu.VMEM)] * len(outs),
        out_shape=[pltpu.VMEM(shape, operand.dtype) for shape in outs],
        scratch_shapes=scratch,
        compiler_params=pltpu.CompilerParams(vmem_limit_bytes=8 << 20),
        cost_estimate=pl.CostEstimate(flops=size, bytes_accessed=4 * size, transcendentals=0),
    )(pltpu.with_memory_space_constraint(operand, space))


def split_rows(gradient):
    rows, cols = gradient.shape
    shape = (4, rows // 2, cols // 16)
    first, others, landed = call(
        theirs_kernel,
        gradient,
        pltpu.HBM,
        [shape, (4, *shape), gradient.shape],
        [pltpu.SemaphoreType.DMA((8,))],
    )
    first, others, landed = lax.optimization_barrier((first, others, landed))
    (own,) = call(own_kernel, landed, pltpu.VMEM, [(4, *shape)])
    return first, others, own


def reduce_blocks(gradient):
    tile = gradient.shape[0] // 2
    x, y, z, core = place()

    first, others, own = split_rows(gradient)
    first, others = swap(first, CORE, CORE), swap(others, CORE, CORE)

    def pair(d):
        return own[d].astype(jnp.float32) + (first if d == 3 else others[d]).astype(jnp.float32)

    over_xy, over_z = (0, Y, X, X + Y), (0, Z_NEAR, Z_FAR, Z_NEAR + Z_FAR)
    sent = {3: narrow(pair(3))}
    own, sent[3] = lax.optimization_barrier((own, sent[3]))
    sent.update({d: narrow(pair(d)) for d in (1, 2)})
    got = [swap(sent[d], over_xy[d], over_z[d ^ (d // 2)]) for d in (3, 1, 2)]
    quarter = lax.optimization_barrier(pair(0) + widen(got[0]))
    quarter = quarter + widen(got[1]) + widen(got[2])
    me = jnp.where(core == 0, z, 2 * x + y)
    got = [swap(narrow(pick(quarter, me ^ d)), over_z[d], over_xy[d]) for d in (1, 2, 3)]
    total = pick(quarter, me) + widen(got[0]) + widen(got[1]) + widen(got[2])

    return jnp.concatenate([total[: tile // 2], total[tile // 2 :]], axis=1)


def join_kernel(mine, far, corner, cross, side, other_side, whole, left):
    cols = mine.shape[1]
    me, core = lax.axis_index("hst"), place()[3]
    bits = lambda at_0, at_1: jnp.where(core == 0, at_0, at_1)
    pieces = [(0, mine), (4, far), (bits(3, 7), corner), (bits(7, 3), cross)]
    pieces += [(bits(2, 1) + 4 * i, side.at[i]) for i in (0, 1)]
    pieces += [(bits(1, 2) + 4 * i, other_side.at[i]) for i in (0, 1)]
    copies = []
    for i, (away, block) in enumerate(pieces):
        at = pl.multiple_of((me ^ away) * cols, 128)
        copies.append(pltpu.make_async_copy(block, whole.at[:, pl.ds(at, cols)], left.at[i]))
        copies[-1].start()
    for copy in copies:
        copy.wait()


def gather_blocks(mine):
    row_block, col_block = mine.shape
    far = swap(mine, Z_FAR, Z_FAR)
    corner, cross = swap(mine, Z_NEAR + Y, Z_FAR + Z_NEAR + Y), swap(mine, Z_FAR + Z_NEAR + Y, Z_NEAR + Y)
    pair = jnp.stack([mine, far])
    side, other_side = swap(pair, Z_NEAR, Y), swap(pair, Y, Z_NEAR)
    whole = pl.pallas_call(
        join_kernel,
        in_specs=[pl.BlockSpec(memory_space=pl.ANY)] * 6,
        out_specs=pl.BlockSpec(memory_space=pl.ANY),
        out_shape=jax.ShapeDtypeStruct((row_block, 8 * col_block), mine.dtype),
        scratch_shapes=[pltpu.SemaphoreType.DMA((8,))],
        compiler_params=pltpu.CompilerParams(vmem_limit_bytes=8 << 20),
        cost_estimate=pl.CostEstimate(flops=0, bytes_accessed=4 * 8 * mine.size, transcendentals=0),
    )(mine, far, corner, cross, side, other_side)
    return whole, corner


def reduce_general(gradient):
    local_count = lax.axis_size("local")
    host_count = lax.axis_size("hst")
    rows, cols = gradient.shape
    row_block, col_block = rows // local_count, cols // host_count
    pieces = lax.all_to_all(
        gradient.reshape(local_count, row_block, cols),
        "local",
        split_axis=0,
        concat_axis=0,
        tiled=True,
    )
    partial_sum = jnp.sum(pieces.astype(jnp.float32), axis=0)
    arrived = lax.all_to_all(
        partial_sum.reshape(row_block, host_count, col_block),
        "hst",
        split_axis=1,
        concat_axis=1,
        tiled=True,
    )
    return jnp.sum(arrived, axis=1)


def adam(grad_total, master, moment_one, moment_two):
    new_one = beta_one * moment_one + (1.0 - beta_one) * grad_total
    new_two = beta_two * moment_two + (1.0 - beta_two) * grad_total * grad_total
    update = new_one / correct_one / (jnp.sqrt(new_two / correct_two) + epsilon)
    new_master = master - learn_rate * (update + decay_rate * master)
    return new_master, new_one, new_two


def local(grads, master, moment_one, moment_two):
    tuned = lax.axis_size("local") == 4 and lax.axis_size("hst") == 8
    gradient = grads[0, 0]
    grad_total = reduce_blocks(gradient) if tuned else reduce_general(gradient)
    mine = adam(grad_total, master, moment_one, moment_two)[0].astype(jnp.bfloat16)
    if tuned:
        secondary, corner = gather_blocks(mine)
    else:
        secondary = corner = lax.all_gather(mine, "hst", axis=1, tiled=True)
    grad_total, _ = lax.optimization_barrier((grad_total, corner))
    new_master, new_one, new_two = adam(grad_total, master, moment_one, moment_two)
    return (grad_total, new_master, new_one, new_two, secondary)


def solution(mesh):
    return jax.shard_map(
        local,
        mesh=mesh,
        in_specs=(
            P("hst", "local", None, None),
            P("local", "hst"),
            P("local", "hst"),
            P("local", "hst"),
        ),
        out_specs=(
            P("local", "hst"),
            P("local", "hst"),
            P("local", "hst"),
            P("local", "hst"),
            P("local", None),
        ),
        check_vma=False,
    )
```

```python
import jax
import jax.numpy as jnp
from jax import lax
from jax.experimental import pallas as pl
from jax.experimental.pallas import tpu as pltpu
from jax.sharding import PartitionSpec as P

beta_one = 0.9
beta_two = 0.95
learn_rate = 0.02
decay_rate = 0.1
epsilon = 1e-08
correct_one = 1.0 - (0.9**50) ** 2
correct_two = 1.0 - (0.95**50) ** 2

wire_scale = 4096.0


def flip_pairs(flips):
    count = lax.axis_size("hst") * lax.axis_size("local")
    return [(i, i ^ flips[i % 2]) for i in range(count)]


def swap(value, *flips):
    return lax.ppermute(value, ("hst", "local"), flip_pairs(flips))


def narrow(value):
    return (value * wire_scale).astype(jnp.float16)


def widen(value):
    return value.astype(jnp.float32) * (1.0 / wire_scale)


def pick(value, index):
    return lax.dynamic_index_in_dim(value, index, 0, keepdims=False)


CORE, X, Y, Z_NEAR, Z_FAR = 1, 2, 4, 8, 16


def place():
    me_local, me_host = lax.axis_index("local"), lax.axis_index("hst")
    return me_local // 2, me_host % 2, me_host // 2, me_local % 2


def rows_of(core, block, i, store):
    tile, half = block.shape[0] // 2, block.shape[1] // 2
    my_x, my_y, my_z, _ = place()
    z, y = i // 2, i % 2
    block = block.astype(jnp.float32)
    for x in (0, 1):
        left, right = block[x * tile : (x + 1) * tile, :half], block[x * tile : (x + 1) * tile, half:]
        rows = [
            jnp.concatenate([left[at : at + tile // 2], right[at : at + tile // 2]], axis=0).astype(jnp.bfloat16)
            for at in (0, tile // 2)
        ]
        over_z = my_z ^ z
        step = jnp.where(core == 0, (2 * my_x + my_y) ^ (2 * x + y), over_z ^ (over_z // 2))
        member = jnp.where(core == 0, z, 2 * x + y)
        store(step, member, jnp.where(core == 0, rows[0], rows[1]))


def theirs_kernel(whole, first, every, landed, arrived):
    half = first.shape[2]
    core = place()[3]
    parts = [pl.ds(2 * i * half, 2 * half) for i in range(8)]
    copies = [
        pltpu.make_async_copy(whole.at[:, part], landed.at[:, part], arrived.at[i])
        for i, part in enumerate(parts)
    ]
    for copy in copies:
        copy.start()

    def store(step, member, rows):
        every[step, member] = rows

    for i in range(8):
        copies[i].wait()
        rows_of(1 - core, landed[:, parts[i]], i, store)
    first[...] = every[3]


def own_kernel(landed, own):
    half = own.shape[3]
    core = place()[3]

    def store(step, member, rows):
        own[step, member] = rows

    for i in range(8):
        rows_of(core, landed[:, pl.ds(2 * i * half, 2 * half)], i, store)


def call(kernel, operand, space, outs, scratch=()):
    size = operand.size
    return pl.pallas_call(
        kernel,
        in_specs=[pl.BlockSpec(memory_space=space)],
        out_specs=[pl.BlockSpec(memory_space=pltpu.VMEM)] * len(outs),
        out_shape=[pltpu.VMEM(shape, operand.dtype) for shape in outs],
        scratch_shapes=scratch,
        compiler_params=pltpu.CompilerParams(vmem_limit_bytes=8 << 20),
        cost_estimate=pl.CostEstimate(flops=size, bytes_accessed=4 * size, transcendentals=0),
    )(pltpu.with_memory_space_constraint(operand, space))


def split_rows(gradient):
    rows, cols = gradient.shape
    shape = (4, rows // 2, cols // 16)
    first, others, landed = call(
        theirs_kernel,
        gradient,
        pltpu.HBM,
        [shape, (4, *shape), gradient.shape],
        [pltpu.SemaphoreType.DMA((8,))],
    )
    first, others, landed = lax.optimization_barrier((first, others, landed))
    (own,) = call(own_kernel, landed, pltpu.VMEM, [(4, *shape)])
    return first, others, own


def reduce_blocks(gradient):
    tile = gradient.shape[0] // 2
    x, y, z, core = place()

    first, others, own = split_rows(gradient)
    first, others = swap(first, CORE, CORE), swap(others, CORE, CORE)

    def pair(d):
        return own[d].astype(jnp.float32) + (first if d == 3 else others[d]).astype(jnp.float32)

    over_xy, over_z = (0, Y, X, X + Y), (0, Z_NEAR, Z_FAR, Z_NEAR + Z_FAR)
    sent = {3: narrow(pair(3))}
    own, sent[3] = lax.optimization_barrier((own, sent[3]))
    sent.update({d: narrow(pair(d)) for d in (1, 2)})
    got = [swap(sent[d], over_xy[d], over_z[d ^ (d // 2)]) for d in (3, 2, 1)]
    quarter = lax.optimization_barrier(pair(0) + widen(got[0]))
    quarter = quarter + widen(got[1]) + widen(got[2])
    me = jnp.where(core == 0, z, 2 * x + y)
    got = [swap(narrow(pick(quarter, me ^ d)), over_z[d], over_xy[d]) for d in (3, 1, 2)]
    total = pick(quarter, me) + widen(got[0]) + widen(got[1]) + widen(got[2])

    return jnp.concatenate([total[: tile // 2], total[tile // 2 :]], axis=1)


def join_kernel(mine, far, corner, cross, side, other_side, whole, left):
    cols = mine.shape[1]
    me, core = lax.axis_index("hst"), place()[3]
    bits = lambda at_0, at_1: jnp.where(core == 0, at_0, at_1)
    pieces = [(0, mine), (4, far), (bits(7, 3), corner), (bits(3, 7), cross)]
    pieces += [(bits(1, 2) + 4 * i, side.at[i]) for i in (0, 1)]
    pieces += [(bits(2, 1) + 4 * i, other_side.at[i]) for i in (0, 1)]
    copies = []
    for i, (away, block) in enumerate(pieces):
        at = pl.multiple_of((me ^ away) * cols, 128)
        copies.append(pltpu.make_async_copy(block, whole.at[:, pl.ds(at, cols)], left.at[i]))
        copies[-1].start()
    for copy in copies:
        copy.wait()


def gather_blocks(mine):
    row_block, col_block = mine.shape
    far = swap(mine, Z_FAR, Z_FAR)
    corner, cross = swap(mine, Z_FAR + Z_NEAR + Y, Z_NEAR + Y), swap(mine, Z_NEAR + Y, Z_FAR + Z_NEAR + Y)
    pair = jnp.stack([mine, far])
    side, other_side = swap(pair, Y, Z_NEAR), swap(pair, Z_NEAR, Y)
    whole = pl.pallas_call(
        join_kernel,
        in_specs=[pl.BlockSpec(memory_space=pl.ANY)] * 6,
        out_specs=pl.BlockSpec(memory_space=pl.ANY),
        out_shape=jax.ShapeDtypeStruct((row_block, 8 * col_block), mine.dtype),
        scratch_shapes=[pltpu.SemaphoreType.DMA((8,))],
        compiler_params=pltpu.CompilerParams(vmem_limit_bytes=8 << 20),
        cost_estimate=pl.CostEstimate(flops=0, bytes_accessed=4 * 8 * mine.size, transcendentals=0),
    )(mine, far, corner, cross, side, other_side)
    return whole, corner


def reduce_general(gradient):
    local_count = lax.axis_size("local")
    host_count = lax.axis_size("hst")
    rows, cols = gradient.shape
    row_block, col_block = rows // local_count, cols // host_count
    pieces = lax.all_to_all(
        gradient.reshape(local_count, row_block, cols),
        "local",
        split_axis=0,
        concat_axis=0,
        tiled=True,
    )
    partial_sum = jnp.sum(pieces.astype(jnp.float32), axis=0)
    arrived = lax.all_to_all(
        partial_sum.reshape(row_block, host_count, col_block),
        "hst",
        split_axis=1,
        concat_axis=1,
        tiled=True,
    )
    return jnp.sum(arrived, axis=1)


def adam(grad_total, master, moment_one, moment_two):
    new_one = beta_one * moment_one + (1.0 - beta_one) * grad_total
    new_two = beta_two * moment_two + (1.0 - beta_two) * grad_total * grad_total
    update = new_one / correct_one / (jnp.sqrt(new_two / correct_two) + epsilon)
    new_master = master - learn_rate * (update + decay_rate * master)
    return new_master, new_one, new_two


def local(grads, master, moment_one, moment_two):
    tuned = lax.axis_size("local") == 4 and lax.axis_size("hst") == 8
    gradient = grads[0, 0]
    grad_total = reduce_blocks(gradient) if tuned else reduce_general(gradient)
    mine = adam(grad_total, master, moment_one, moment_two)[0].astype(jnp.bfloat16)
    if tuned:
        secondary, corner = gather_blocks(mine)
    else:
        secondary = corner = lax.all_gather(mine, "hst", axis=1, tiled=True)
    grad_total, _ = lax.optimization_barrier((grad_total, corner))
    new_master, new_one, new_two = adam(grad_total, master, moment_one, moment_two)
    return (grad_total, new_master, new_one, new_two, secondary)


def solution(mesh):
    return jax.shard_map(
        local,
        mesh=mesh,
        in_specs=(
            P("hst", "local", None, None),
            P("local", "hst"),
            P("local", "hst"),
            P("local", "hst"),
        ),
        out_specs=(
            P("local", "hst"),
            P("local", "hst"),
            P("local", "hst"),
            P("local", "hst"),
            P("local", None),
        ),
        check_vma=False,
    )
```

```python
import jax
import jax.numpy as jnp
from jax import lax
from jax.experimental import pallas as pl
from jax.experimental.pallas import tpu as pltpu
from jax.sharding import PartitionSpec as P

beta_one = 0.9
beta_two = 0.95
learn_rate = 0.02
decay_rate = 0.1
epsilon = 1e-08
correct_one = 1.0 - (0.9**50) ** 2
correct_two = 1.0 - (0.95**50) ** 2

wire_scale = 4096.0


def flip_pairs(flips):
    count = lax.axis_size("hst") * lax.axis_size("local")
    return [(i, i ^ flips[i % 2]) for i in range(count)]


def swap(value, *flips):
    return lax.ppermute(value, ("hst", "local"), flip_pairs(flips))


def narrow(value):
    return (value * wire_scale).astype(jnp.float16)


def widen(value):
    return value.astype(jnp.float32) * (1.0 / wire_scale)


def pick(value, index):
    return lax.dynamic_index_in_dim(value, index, 0, keepdims=False)


CORE, X, Y, Z_NEAR, Z_FAR = 1, 2, 4, 8, 16


def place():
    me_local, me_host = lax.axis_index("local"), lax.axis_index("hst")
    return me_local // 2, me_host % 2, me_host // 2, me_local % 2


def rows_of(core, block, i, store):
    tile, half = block.shape[0] // 2, block.shape[1] // 2
    my_x, my_y, my_z, _ = place()
    z, y = i // 2, i % 2
    block = block.astype(jnp.float32)
    for x in (0, 1):
        left, right = block[x * tile : (x + 1) * tile, :half], block[x * tile : (x + 1) * tile, half:]
        rows = [
            jnp.concatenate([left[at : at + tile // 2], right[at : at + tile // 2]], axis=0).astype(jnp.bfloat16)
            for at in (0, tile // 2)
        ]
        over_z = my_z ^ z
        step = jnp.where(core == 0, (2 * my_x + my_y) ^ (2 * x + y), over_z ^ (over_z // 2))
        member = jnp.where(core == 0, z, 2 * x + y)
        store(step, member, jnp.where(core == 0, rows[0], rows[1]))


def theirs_kernel(whole, first, every, landed, arrived):
    half = first.shape[2]
    core = place()[3]
    parts = [pl.ds(4 * i * half, 4 * half) for i in range(4)]
    copies = [
        pltpu.make_async_copy(whole.at[:, part], landed.at[:, part], arrived.at[i])
        for i, part in enumerate(parts)
    ]
    for copy in copies:
        copy.start()

    def store(step, member, rows):
        every[step, member] = rows

    for i in range(8):
        if i % 2 == 0:
            copies[i // 2].wait()
        rows_of(1 - core, landed[:, pl.ds(2 * i * half, 2 * half)], i, store)
    first[...] = every[3]


def own_kernel(landed, own):
    half = own.shape[3]
    core = place()[3]

    def store(step, member, rows):
        own[step, member] = rows

    for i in range(8):
        rows_of(core, landed[:, pl.ds(2 * i * half, 2 * half)], i, store)


def call(kernel, operand, space, outs, scratch=()):
    size = operand.size
    return pl.pallas_call(
        kernel,
        in_specs=[pl.BlockSpec(memory_space=space)],
        out_specs=[pl.BlockSpec(memory_space=pltpu.VMEM)] * len(outs),
        out_shape=[pltpu.VMEM(shape, operand.dtype) for shape in outs],
        scratch_shapes=scratch,
        compiler_params=pltpu.CompilerParams(vmem_limit_bytes=8 << 20),
        cost_estimate=pl.CostEstimate(flops=size, bytes_accessed=4 * size, transcendentals=0),
    )(pltpu.with_memory_space_constraint(operand, space))


def split_rows(gradient):
    rows, cols = gradient.shape
    shape = (4, rows // 2, cols // 16)
    first, others, landed = call(
        theirs_kernel,
        gradient,
        pltpu.HBM,
        [shape, (4, *shape), gradient.shape],
        [pltpu.SemaphoreType.DMA((4,))],
    )
    first, others, landed = lax.optimization_barrier((first, others, landed))
    (own,) = call(own_kernel, landed, pltpu.VMEM, [(4, *shape)])
    return first, others, own


def reduce_blocks(gradient):
    tile = gradient.shape[0] // 2
    x, y, z, core = place()

    first, others, own = split_rows(gradient)
    first, others = swap(first, CORE, CORE), swap(others, CORE, CORE)

    def pair(d):
        return own[d].astype(jnp.float32) + (first if d == 3 else others[d]).astype(jnp.float32)

    over_xy, over_z = (0, Y, X, X + Y), (0, Z_NEAR, Z_FAR, Z_NEAR + Z_FAR)
    sent = {3: narrow(pair(3))}
    own, sent[3] = lax.optimization_barrier((own, sent[3]))
    sent.update({d: narrow(pair(d)) for d in (1, 2)})
    got = [swap(sent[d], over_xy[d], over_z[d ^ (d // 2)]) for d in (3, 2, 1)]
    quarter = lax.optimization_barrier(pair(0) + widen(got[0]))
    quarter = quarter + widen(got[1]) + widen(got[2])
    me = jnp.where(core == 0, z, 2 * x + y)
    got = [swap(narrow(pick(quarter, me ^ d)), over_z[d], over_xy[d]) for d in (3, 1, 2)]
    total = pick(quarter, me) + widen(got[0]) + widen(got[1]) + widen(got[2])

    return jnp.concatenate([total[: tile // 2], total[tile // 2 :]], axis=1)


def join_kernel(mine, far, corner, cross, side, other_side, whole, left):
    cols = mine.shape[1]
    me, core = lax.axis_index("hst"), place()[3]
    bits = lambda at_0, at_1: jnp.where(core == 0, at_0, at_1)
    pieces = [(0, mine), (4, far), (bits(7, 3), corner), (bits(3, 7), cross)]
    pieces += [(bits(1, 2) + 4 * i, side.at[i]) for i in (0, 1)]
    pieces += [(bits(2, 1) + 4 * i, other_side.at[i]) for i in (0, 1)]
    copies = []
    for i, (away, block) in enumerate(pieces):
        at = pl.multiple_of((me ^ away) * cols, 128)
        copies.append(pltpu.make_async_copy(block, whole.at[:, pl.ds(at, cols)], left.at[i]))
        copies[-1].start()
    for copy in copies:
        copy.wait()


def gather_blocks(mine):
    row_block, col_block = mine.shape
    far = swap(mine, Z_FAR, Z_FAR)
    corner, cross = swap(mine, Z_FAR + Z_NEAR + Y, Z_NEAR + Y), swap(mine, Z_NEAR + Y, Z_FAR + Z_NEAR + Y)
    pair = jnp.stack([mine, far])
    side, other_side = swap(pair, Y, Z_NEAR), swap(pair, Z_NEAR, Y)
    whole = pl.pallas_call(
        join_kernel,
        in_specs=[pl.BlockSpec(memory_space=pl.ANY)] * 6,
        out_specs=pl.BlockSpec(memory_space=pl.ANY),
        out_shape=jax.ShapeDtypeStruct((row_block, 8 * col_block), mine.dtype),
        scratch_shapes=[pltpu.SemaphoreType.DMA((8,))],
        compiler_params=pltpu.CompilerParams(vmem_limit_bytes=8 << 20),
        cost_estimate=pl.CostEstimate(flops=0, bytes_accessed=4 * 8 * mine.size, transcendentals=0),
    )(mine, far, corner, cross, side, other_side)
    return whole, corner


def reduce_general(gradient):
    local_count = lax.axis_size("local")
    host_count = lax.axis_size("hst")
    rows, cols = gradient.shape
    row_block, col_block = rows // local_count, cols // host_count
    pieces = lax.all_to_all(
        gradient.reshape(local_count, row_block, cols),
        "local",
        split_axis=0,
        concat_axis=0,
        tiled=True,
    )
    partial_sum = jnp.sum(pieces.astype(jnp.float32), axis=0)
    arrived = lax.all_to_all(
        partial_sum.reshape(row_block, host_count, col_block),
        "hst",
        split_axis=1,
        concat_axis=1,
        tiled=True,
    )
    return jnp.sum(arrived, axis=1)


def adam(grad_total, master, moment_one, moment_two):
    new_one = beta_one * moment_one + (1.0 - beta_one) * grad_total
    new_two = beta_two * moment_two + (1.0 - beta_two) * grad_total * grad_total
    update = new_one / correct_one / (jnp.sqrt(new_two / correct_two) + epsilon)
    new_master = master - learn_rate * (update + decay_rate * master)
    return new_master, new_one, new_two


def local(grads, master, moment_one, moment_two):
    tuned = lax.axis_size("local") == 4 and lax.axis_size("hst") == 8
    gradient = grads[0, 0]
    grad_total = reduce_blocks(gradient) if tuned else reduce_general(gradient)
    mine = adam(grad_total, master, moment_one, moment_two)[0].astype(jnp.bfloat16)
    if tuned:
        secondary, corner = gather_blocks(mine)
    else:
        secondary = corner = lax.all_gather(mine, "hst", axis=1, tiled=True)
    grad_total, _ = lax.optimization_barrier((grad_total, corner))
    new_master, new_one, new_two = adam(grad_total, master, moment_one, moment_two)
    return (grad_total, new_master, new_one, new_two, secondary)


def solution(mesh):
    return jax.shard_map(
        local,
        mesh=mesh,
        in_specs=(
            P("hst", "local", None, None),
            P("local", "hst"),
            P("local", "hst"),
            P("local", "hst"),
        ),
        out_specs=(
            P("local", "hst"),
            P("local", "hst"),
            P("local", "hst"),
            P("local", "hst"),
            P("local", None),
        ),
        check_vma=False,
    )
```
